512 devices in a mesh: seq: 64 (over y, x, core), mp: 8 (over z).
Axes of the slice: x: 4, y: 8, z: 8, core: 2. Of those that a mesh axis runs over, the one named last changes fastest.
Arguments:
- tokens: bfloat16 [32768, 4096], P('seq', 'mp'), may hold values from -6 to 6
- x_gain: bfloat16 [4096], P('mp'), may hold values from 0.099609375 to 1.8984375
- w_router: bfloat16 [4096], P('mp'), may hold values from -0.09375 to 0.09375
- w_query: bfloat16 [4096, 4096], P('seq', 'mp'), may hold values from -0.09375 to 0.09375
- key_weight: bfloat16 [4096, 1024], P('seq', 'mp'), may hold values from -0.09375 to 0.09375
- value_weight: bfloat16 [4096, 1024], P('seq', 'mp'), may hold values from -0.09375 to 0.09375
- q_gain: float32 [128], replicated, may hold values from 1 to 3
- key_norm_gain: float32 [128], replicated, may hold values from 0.1 to 1.9
- route_pos: int32 [12288], P('seq'), may hold values from 0 to 511, as said below
- route_count: int32 [64], P('seq'), may hold values from 1 to 192, 4096 in all
Outputs:
- attended: bfloat16 [32768, 4096], P('seq', 'mp')
The draws below stay inside these ranges and needn't reach their ends.
Inputs may be any that keep to these rules, and one draw needn't show every extreme that they name: The counts of all devices sum to exactly 4096; device s routes the positions in the first route_count[s] of its 192 slots of route_pos. `route_pos`: within one device's 192 slots the positions are distinct; they index positions of that device's block of 512.
All inputs are finite; a program needn't handle non-finite values.
Results may differ from the reference program's by a relative error of at most 0.011.
Values may be sent and summed in bfloat16 or wider, within the bound.
No kernel may reach another device: no remote copies, remote signals or barrier semaphores. Data moves between devices by JAX's collectives and lax.ppermute only.
A program may use at most 128 MiB of HBM per device.

```python
import math
import jax
import jax.numpy as jnp
import numpy as np
from jax import lax

D = 4096
QUERY_HEADS = 32
KEY_VALUE_HEADS = 8
HEAD_DIMENSION = 128
TOK_DEV = 512
CAP = 192
TOKENS = 32768
SLOTS = 12288
QW = 4096
KW = 1024
N_SEQ = 64


def draw_route_pos(key, part):
    key = jax.random.fold_in(key, 11)
    partition_total = SLOTS // CAP
    attention_logits = jax.random.randint(key, (partition_total, TOK_DEV), 0, 1 << 19)
    edges = jnp.zeros((partition_total, TOK_DEV), jnp.int32).at[0, 0].set(1 << 19).at[0, TOK_DEV - 1].set(1 << 19)
    ranked = (attention_logits + edges) * TOK_DEV + jnp.arange(TOK_DEV, dtype=jnp.int32)[None, :]
    chosen = lax.top_k(ranked, CAP)[1]
    return chosen.astype(jnp.int32).reshape(-1)


def level_of(key, extent, shards, least, largest):
    level, own = 1.0, jax.random.fold_in(key, 6)
    for axis_at, blocks in shards:
        heights = jnp.exp(jax.random.uniform(jax.random.fold_in(own, axis_at), (blocks,), jnp.float32, least / len(shards), largest / len(shards)))
        level = level * jnp.repeat(heights, extent[axis_at] // blocks).reshape([-1 if axis == axis_at else 1 for axis in range(len(extent))])
    return level


def split_up(number_of, total, reach, lean):
    loads = [(1 << 20) // math.isqrt(standing ** lean) + 1 for standing in range(2, number_of + 1)]
    rest, given = total - reach - (number_of - 1), [1] * (number_of - 1)
    while rest > 0:
        candidates = [i for i in range(number_of - 1) if given[i] < reach]
        whole, remaining = sum([loads[i] for i in candidates]), rest
        for i in candidates:
            addition = min(reach - given[i], max(1, remaining * loads[i] // whole), rest)
            given[i] = given[i] + addition
            rest = rest - addition
    return np.array([reach] + given)


def ragged(own_key, count, total, most, slope):
    if count == 2:
        one = jax.random.randint(own_key, (), max(1, total - most), min(most, total - 1) + 1)
        return jnp.stack([one, total - one])
    lengths = jnp.asarray(split_up(count, total, most, slope), jnp.int32)
    pairs = (count - 1) // 2
    donor, sink = lengths[1:1 + 2 * pairs:2], lengths[2:2 + 2 * pairs:2]
    slack = jnp.minimum(donor - 1, most - sink)
    passed = jax.random.randint(jax.random.fold_in(own_key, 1), (pairs,), 0, 1 << 20) % (slack + 1)
    lengths = lengths.at[1:1 + 2 * pairs:2].set(donor - passed).at[2:2 + 2 * pairs:2].set(sink + passed)
    return lengths[jax.random.permutation(jax.random.fold_in(own_key, 2), count)]


def centred(own_key, extent, spread, most, shards=(), kind=jnp.bfloat16):
    values = jax.random.normal(own_key, extent, jnp.float32) * spread
    if len(shards) > 0:
        values = level_of(own_key, extent, shards, -0.22, 0.18) * values
    return jnp.clip(values, min=-most, max=most).astype(kind)


def setup_inputs(seed: int = 0) -> dict:
    splits = jax.random.split(jax.random.key(seed), 11)
    return {
        "tokens": centred(splits[0], (TOKENS, D), 1.0, 6.0, ((0, 64), (1, 8))),
        "x_gain": jnp.clip(1.0 + 0.18 * jax.random.normal(splits[1], (D,), jnp.float32), 0.099609375, 1.8984375).astype(jnp.bfloat16),
        "w_router": centred(splits[2], (D,), D ** -0.5, 0.09375, ((0, 8),)),
        "w_query": centred(splits[3], (D, QW), D ** -0.5, 0.09375, ((0, 64), (1, 8))),
        "key_weight": centred(splits[4], (D, KW), D ** -0.5, 0.09375, ((0, 64), (1, 8))),
        "value_weight": centred(splits[5], (D, KW), D ** -0.5, 0.09375, ((0, 64), (1, 8))),
        "q_gain": jnp.clip(jnp.exp(jax.random.uniform(splits[6], (HEAD_DIMENSION,), jnp.float32, math.log(1.0), math.log(3.0))), 1.0, 3.0),
        "key_norm_gain": jnp.clip(1.0 + 0.18 * jax.random.normal(splits[7], (HEAD_DIMENSION,), jnp.float32), 0.1, 1.9),
        "route_pos": draw_route_pos(jax.random.fold_in(splits[10], 71), 0),
        "route_count": ragged(splits[9], N_SEQ, TOKENS // 8, CAP, 2).astype(jnp.int32),
    }


def per_head_norm(projected, gain):
    mean_sq = lax.optimization_barrier(jnp.mean(projected * projected, axis=-1, keepdims=True))
    return (projected * lax.rsqrt(mean_sq + 1e-06) * gain.astype(jnp.float32)).astype(jnp.bfloat16)

def reference(tokens, x_gain, w_router, w_query, key_weight, value_weight, q_gain, key_norm_gain, route_pos, route_count):
    partition_total = route_count.shape[0]
    slot_capacity = route_pos.shape[0] // partition_total
    slot_index = jnp.arange(slot_capacity, dtype=jnp.int32)
    shard_base = jnp.arange(partition_total, dtype=jnp.int32)[:, None] * TOK_DEV
    local_pos = route_pos.reshape(partition_total, slot_capacity)
    routed = slot_index[None, :] < route_count[:, None]
    source_pos = (shard_base + local_pos).reshape(-1).astype(jnp.int32)
    positions = jnp.where(routed.reshape(-1), source_pos, -1).astype(jnp.int32)
    count_of_rows = source_pos.shape[0]
    widened = tokens[source_pos].astype(jnp.float32)
    mean_sq = lax.optimization_barrier(jnp.mean(widened * widened, axis=-1, keepdims=True))
    normalized_rows = (widened * lax.rsqrt(mean_sq + 1e-05) * x_gain.astype(jnp.float32)).astype(jnp.bfloat16)
    router_gate = jax.nn.sigmoid(jnp.dot(normalized_rows, w_router, preferred_element_type=jnp.float32))
    query_matrix = per_head_norm(jnp.dot(normalized_rows, w_query, preferred_element_type=jnp.float32).reshape(count_of_rows, QUERY_HEADS, HEAD_DIMENSION), q_gain)
    key_matrix = per_head_norm(jnp.dot(normalized_rows, key_weight, preferred_element_type=jnp.float32).reshape(count_of_rows, KEY_VALUE_HEADS, HEAD_DIMENSION), key_norm_gain)
    value_matrix = jnp.dot(normalized_rows, value_weight, preferred_element_type=jnp.float32).astype(jnp.bfloat16).reshape(count_of_rows, KEY_VALUE_HEADS, HEAD_DIMENSION)
    key_expanded = key_matrix.astype(jnp.float32)
    value_expanded = value_matrix.astype(jnp.float32)
    logit_scale = 1.0 / math.sqrt(HEAD_DIMENSION)
    grouped_heads = query_matrix.reshape(partition_total, slot_capacity, KEY_VALUE_HEADS, QUERY_HEADS // KEY_VALUE_HEADS, HEAD_DIMENSION)

    def attend_block(block):
        query_tile_block, query_pos = block
        attention_logits = jnp.einsum('iqef,oqf->iqeo', query_tile_block.astype(jnp.float32), key_expanded) * logit_scale
        allowed = (positions[None, :] >= 0) & (positions[None, :] <= query_pos[:, None])
        weights = jnp.where(allowed[:, None, None, :], jnp.exp(attention_logits), 0.0)
        softmax_divisor = lax.optimization_barrier(jnp.sum(weights, axis=-1))
        rounded_up = lax.optimization_barrier(weights.astype(jnp.bfloat16)).astype(jnp.float32)
        softmax_dividend = jnp.einsum('vtme,eti->vtmi', rounded_up, value_expanded)
        return (softmax_dividend, softmax_divisor)
    softmax_dividend, softmax_divisor = lax.map(attend_block, (grouped_heads, positions.reshape(partition_total, slot_capacity)))
    softmax_dividend = softmax_dividend.reshape(count_of_rows, KEY_VALUE_HEADS, QUERY_HEADS // KEY_VALUE_HEADS, HEAD_DIMENSION)
    softmax_divisor = softmax_divisor.reshape(count_of_rows, KEY_VALUE_HEADS, QUERY_HEADS // KEY_VALUE_HEADS)
    is_live = positions >= 0
    safe_total = jnp.where(is_live[:, None, None], softmax_divisor, 1.0)
    attended = (router_gate[:, None, None, None] * softmax_dividend / safe_total[..., None]).reshape(count_of_rows, QUERY_HEADS * HEAD_DIMENSION).astype(jnp.bfloat16)
    target = jnp.where(is_live, positions, TOKENS).astype(jnp.int32)
    return jnp.zeros((TOKENS, QUERY_HEADS * HEAD_DIMENSION), jnp.bfloat16).at[target].set(attended, mode='drop')
```

```python
import math

import jax
import jax.numpy as jnp
from jax import lax
from jax.experimental import pallas as pl
from jax.experimental.pallas import tpu as pltpu
from jax.sharding import Mesh
from jax.sharding import PartitionSpec as P

PLANE = ("y", "x")
SEQ = ("y", "x", "core")
TILE = 512
VMEM_BYTES = 56 * 1024 * 1024


def whole(memory_space=pltpu.VMEM):
    return pl.BlockSpec(memory_space=memory_space)


def params():
    return pltpu.CompilerParams(vmem_limit_bytes=VMEM_BYTES)


def dot(a, b, contract_a=1, contract_b=0):
    return lax.dot_general(
        a, b, (((contract_a,), (contract_b,)), ((), ())), preferred_element_type=jnp.float32
    )


def pick_rows_kernel(tokens_ref, pos_ref, gain_ref, router_ref, out_ref):
    slots = pos_ref.shape[1]
    rows, width = tokens_ref.shape
    hit = lax.broadcasted_iota(jnp.int32, (rows, slots), 0) == pos_ref[...]
    one_hot = jnp.where(hit, 1.0, 0.0).astype(jnp.bfloat16)
    out_ref[:slots, :] = dot(one_hot, tokens_ref[...], 0, 0).astype(jnp.bfloat16)
    at = lax.broadcasted_iota(jnp.int32, (out_ref.shape[0] - slots, width), 0)
    extra = jnp.where(at == 0, gain_ref[...].astype(jnp.float32), 0.0)
    extra = jnp.where(at == 1, router_ref[...].astype(jnp.float32), extra)
    out_ref[slots:, :] = extra.astype(jnp.bfloat16)


def pick_rows(tokens, route_pos, x_gain, w_router):
    slots = route_pos.shape[0]
    width = tokens.shape[1]
    return pl.pallas_call(
        pick_rows_kernel,
        out_shape=jax.ShapeDtypeStruct((slots + 16, width), jnp.bfloat16),
        in_specs=[whole()] * 4,
        out_specs=whole(),
        compiler_params=params(),
        name="pick_rows",
    )(tokens, route_pos.reshape(1, slots), x_gain.reshape(1, width), w_router.reshape(1, width))


def head_norm(projected, gain):
    mean_sq = jnp.mean(projected * projected, axis=-1, keepdims=True)
    return (projected * lax.rsqrt(mean_sq + 1e-06) * gain).astype(jnp.bfloat16)


def in_feature_order(core, mine, other):
    even = jnp.where(core == 0, mine, other)
    odd = jnp.where(core == 0, other, mine)
    return jnp.stack([even, odd], axis=1).reshape(-1, mine.shape[-1])


def keys_kernel(place_ref, count_ref, rows_ref, mine_ref, other_ref, gain_ref, xn_ref, kv_ref, gate_ref):
    parts, padded, width = rows_ref.shape
    slots, head = kv_ref.shape[0], gain_ref.shape[1]
    core, count = place_ref[0], count_ref[0]
    square = jnp.zeros((slots, width), jnp.float32)
    for part in range(parts):
        wide = rows_ref[part, :slots, :].astype(jnp.float32)
        square += wide * wide
    mean_sq = jnp.sum(square, axis=-1, keepdims=True) / (parts * width)
    scale = lax.rsqrt(mean_sq + 1e-05)
    total = jnp.zeros((slots, 2 * head), jnp.float32)
    routed = jnp.zeros((slots, width), jnp.float32)
    step = mine_ref.shape[0] // parts
    for part in range(parts):
        extra = rows_ref[part, slots:, :].astype(jnp.float32)
        wide = rows_ref[part, :slots, :].astype(jnp.float32)
        normed = (wide * scale * extra[0:1]).astype(jnp.bfloat16)
        xn_ref[:, part * width : (part + 1) * width] = normed
        routed += normed.astype(jnp.float32) * extra[1:2]
        own = slice(part * step, (part + 1) * step)
        weights = in_feature_order(core, mine_ref[own, :64, :], other_ref[own, :64, :])
        total += dot(normed, weights)
    gate = jax.nn.sigmoid(jnp.sum(routed, axis=-1, keepdims=True))
    gate_ref[...] = jnp.broadcast_to(gate, gate_ref.shape)
    kv_ref[:, :head] = head_norm(total[:, :head], gain_ref[...])
    live = lax.broadcasted_iota(jnp.int32, (slots, head), 0) < count
    kv_ref[:, head:] = jnp.where(live, total[:, head:], 0.0).astype(jnp.bfloat16)


def make_keys(core, count, rows, mine, other, gain, slots):
    parts, _, width = rows.shape
    head = gain.shape[0]
    return pl.pallas_call(
        keys_kernel,
        out_shape=(
            jax.ShapeDtypeStruct((slots, parts * width), jnp.bfloat16),
            jax.ShapeDtypeStruct((slots, 2 * head), jnp.bfloat16),
            jax.ShapeDtypeStruct((slots, head), jnp.float32),
        ),
        in_specs=[whole(pltpu.SMEM)] * 2 + [whole()] * 4,
        out_specs=(whole(),) * 3,
        compiler_params=params(),
        name="make_keys",
    )(core, count, rows, mine, other, gain.reshape(1, head))


def queries_kernel(xn_ref, weights_ref, gain_ref, out_ref):
    blocks, _, width = weights_ref.shape
    slots, head = out_ref.shape[0], gain_ref.shape[1]
    total = jnp.zeros((slots, width), jnp.float32)
    step = 8
    for at in range(0, blocks, step):
        weights = weights_ref[at : at + step, :64, :].reshape(step * 64, width)
        total += dot(xn_ref[:, at * 64 : (at + step) * 64], weights)
    for at in range(0, width, head):
        out_ref[:, at : at + head] = head_norm(total[:, at : at + head], gain_ref[...])


def make_queries(xn, weights, gain):
    return pl.pallas_call(
        queries_kernel,
        out_shape=jax.ShapeDtypeStruct((xn.shape[0], weights.shape[2]), jnp.bfloat16),
        in_specs=[whole()] * 3,
        out_specs=whole(),
        compiler_params=params(),
        name="make_queries",
    )(xn, weights, gain.reshape(1, -1))


def attend_kernel(
    lengths_ref, count_ref, q_ref, own_ref, mine_ref, other_ref, pos_row_ref, pos_col_ref, gate_ref,
    out_ref, packed, total,
):
    slots, head = gate_ref.shape
    group = q_ref.shape[1] // head
    count = count_ref[0]
    factor = math.log2(math.e) / math.sqrt(head)
    fill = lax.broadcasted_iota(jnp.int32, (slots, head), 0)

    def pack(at, offset):
        for which, ref in enumerate((mine_ref, other_ref)):
            length = lengths_ref[which, at]

            @pl.when(length > 0)
            def _():
                where = pl.ds(pl.multiple_of(offset, 16), slots)
                packed[where, : 2 * head] = ref[at, :slots, :]
                packed[where, 2 * head :] = jnp.where(fill < length, 1.0, 0.0).astype(jnp.bfloat16)

            offset = offset + (length + 15) // 16 * 16
        return offset

    end = lax.fori_loop(0, mine_ref.shape[0], pack, jnp.int32(0))
    packed[pl.ds(pl.multiple_of(end, 16), TILE), :] = jnp.zeros((TILE, packed.shape[1]), jnp.bfloat16)

    allowed = (pos_row_ref[...] <= pos_col_ref[...]) & (
        lax.broadcasted_iota(jnp.int32, (slots, slots), 1) < count
    )
    summed = jnp.concatenate([own_ref[:, head:], jnp.ones((slots, head), jnp.bfloat16)], axis=1)
    for h in range(group):
        query = q_ref[:, h * head : (h + 1) * head]
        weights = jnp.exp2(dot(query, own_ref[:, :head], 1, 1) * factor)
        weights = jnp.where(allowed, weights, 0.0).astype(jnp.bfloat16)
        total[h] = dot(weights, summed)

    def tile(at, carry):
        rows = pl.ds(pl.multiple_of(at * TILE, TILE), TILE)
        keys, values = packed[rows, :head], packed[rows, head:]
        for h in range(group):
            query = q_ref[:, h * head : (h + 1) * head]
            weights = jnp.exp2(dot(query, keys, 1, 1) * factor).astype(jnp.bfloat16)
            total[h] += dot(weights, values)
        return carry

    lax.fori_loop(0, (end + TILE - 1) // TILE, tile, 0)

    block = out_ref.shape[0]
    live = fill < count
    pieces = []
    for h in range(group):
        sums = total[h]
        piece = gate_ref[...] * sums[:, :head] / jnp.where(live, sums[:, head:], 1.0)
        pieces.append(jnp.where(live, piece, 0.0).astype(jnp.bfloat16))
    hit = (lax.broadcasted_iota(jnp.int32, (block, slots), 0) == pos_row_ref[...]) & (
        lax.broadcasted_iota(jnp.int32, (block, slots), 1) < count
    )
    one_hot = jnp.where(hit, 1.0, 0.0).astype(jnp.bfloat16)
    out_ref[...] = dot(one_hot, jnp.concatenate(pieces, axis=1)).astype(jnp.bfloat16)


def attend(lengths, count, queries, own, mine, other, route_pos, gate, block):
    slots, width = queries.shape
    head = gate.shape[1]
    sources = 2 * mine.shape[0]
    most = sources * block // 8 + 16 * sources + slots + TILE
    return pl.pallas_call(
        attend_kernel,
        out_shape=jax.ShapeDtypeStruct((block, width), jnp.bfloat16),
        in_specs=[whole(pltpu.SMEM)] * 2 + [whole()] * 7,
        out_specs=whole(),
        scratch_shapes=[
            pltpu.VMEM(((most + TILE - 1) // TILE * TILE, 3 * head), jnp.bfloat16),
            pltpu.VMEM((width // head, slots, 2 * head), jnp.float32),
        ],
        compiler_params=params(),
        name="attend",
    )(lengths, count, queries, own, mine, other, route_pos.reshape(1, slots), route_pos.reshape(slots, 1), gate)


def to_all(block, axes, peers):
    return lax.all_to_all(
        jnp.broadcast_to(block[None], (peers,) + block.shape), axes, 0, 0, tiled=True
    )


def swap_cores(block):
    return lax.ppermute(block, "core", [(0, 1), (1, 0)])


def local(
    tokens, x_gain, w_router, w_query, key_weight, value_weight, q_gain, key_norm_gain, route_pos, route_count
):
    ny, nx, nz = lax.axis_size("y"), lax.axis_size("x"), lax.axis_size("z")
    block = tokens.shape[0]
    slots = route_pos.shape[0]
    core = lax.axis_index("core").astype(jnp.int32)
    shard = lax.axis_index(SEQ).astype(jnp.int32)

    picked = pick_rows(tokens, route_pos, x_gain, w_router)
    rows = lax.all_gather(picked, "z", axis=0, tiled=False)

    key_value = jnp.concatenate([key_weight, value_weight], axis=1)
    kv_mine = to_all(key_value, PLANE, ny * nx)
    kv_other = swap_cores(kv_mine)

    counted = jnp.broadcast_to(route_count.astype(jnp.bfloat16)[:, None], (16, w_query.shape[1]))
    wq = lax.all_gather(jnp.concatenate([w_query, counted], axis=0), SEQ, axis=0, tiled=False)

    normed, kv, gate = make_keys(core[None], route_count, rows, kv_mine, kv_other, key_norm_gain, slots)

    kv_y = lax.all_gather(kv, "y", axis=0, tiled=False)
    kv_yx = to_all(kv_y, "x", nx).reshape(nx * ny, slots, kv.shape[1])
    kv_xy_other = swap_cores(kv_yx)

    queries = make_queries(normed, wq, q_gain)
    counts = wq[:, w_query.shape[0], 0].astype(jnp.int32)
    counts = jnp.where(jnp.arange(counts.shape[0], dtype=jnp.int32) < shard, counts, 0)
    per_core = counts.reshape(ny, nx, 2).transpose(2, 1, 0).reshape(2, nx * ny)
    lengths = jnp.where(core == 0, per_core, per_core[::-1])
    return attend(lengths, route_count, queries, kv, kv_yx, kv_xy_other, route_pos, gate, block)


def solution(mesh):
    grid = Mesh(mesh.devices.reshape(8, 4, 2, 8), ("y", "x", "core", "z"))
    return jax.shard_map(
        local,
        mesh=grid,
        in_specs=(
            P(SEQ, "z"), P("z"), P("z"), P(SEQ, "z"), P(SEQ, "z"), P(SEQ, "z"), P(), P(), P(SEQ), P(SEQ),
        ),
        out_specs=P(SEQ, "z"),
        check_vma=False,
    )
```

```python
import math

import jax
import jax.numpy as jnp
from jax import lax
from jax.experimental import pallas as pl
from jax.experimental.pallas import tpu as pltpu
from jax.sharding import Mesh
from jax.sharding import PartitionSpec as P

PLANE = ("y", "x")
SEQ = ("y", "x", "core")
TILE = 512
VMEM_BYTES = 56 * 1024 * 1024


def whole(memory_space=pltpu.VMEM):
    return pl.BlockSpec(memory_space=memory_space)


def params():
    return pltpu.CompilerParams(vmem_limit_bytes=VMEM_BYTES)


def dot(a, b, contract_a=1, contract_b=0):
    return lax.dot_general(
        a, b, (((contract_a,), (contract_b,)), ((), ())), preferred_element_type=jnp.float32
    )


def pick_rows_kernel(tokens_ref, pos_ref, gain_ref, router_ref, out_ref):
    slots = pos_ref.shape[1]
    rows, width = tokens_ref.shape
    hit = lax.broadcasted_iota(jnp.int32, (rows, slots), 0) == pos_ref[...]
    one_hot = jnp.where(hit, 1.0, 0.0).astype(jnp.bfloat16)
    out_ref[:slots, :] = dot(one_hot, tokens_ref[...], 0, 0).astype(jnp.bfloat16)
    at = lax.broadcasted_iota(jnp.int32, (out_ref.shape[0] - slots, width), 0)
    extra = jnp.where(at == 0, gain_ref[...].astype(jnp.float32).reshape(1, width), 0.0)
    extra = jnp.where(at == 1, router_ref[...].astype(jnp.float32).reshape(1, width), extra)
    out_ref[slots:, :] = extra.astype(jnp.bfloat16)


def pick_rows(tokens, route_pos, x_gain, w_router):
    slots = route_pos.shape[0]
    width = tokens.shape[1]
    return pl.pallas_call(
        pick_rows_kernel,
        out_shape=jax.ShapeDtypeStruct((slots + 16, width), jnp.bfloat16),
        in_specs=[whole()] * 4,
        out_specs=whole(),
        compiler_params=params(),
        name="pick_rows",
    )(tokens, route_pos.reshape(1, slots), x_gain, w_router)


def head_norm(projected, gain):
    mean_sq = jnp.mean(projected * projected, axis=-1, keepdims=True)
    return (projected * lax.rsqrt(mean_sq + 1e-06) * gain).astype(jnp.bfloat16)


def in_feature_order(core, mine, other):
    even = jnp.where(core == 0, mine, other)
    odd = jnp.where(core == 0, other, mine)
    return jnp.stack([even, odd], axis=1).reshape(-1, mine.shape[-1])


def keys_kernel(
    place_ref, count_ref, rows_ref, mine_ref, other_ref, gain_ref, xn_ref, kv_ref, gate_ref, total, routed, scale
):
    parts, _, width = rows_ref.shape
    slots, head = gate_ref.shape
    core, count = place_ref[0], count_ref[0]
    at, steps, each = pl.program_id(0), pl.num_programs(0), mine_ref.shape[1]

    @pl.when(at == 0)
    def _():
        square = jnp.zeros((slots, width), jnp.float32)
        for part in range(parts):
            wide = rows_ref[part, :slots, :].astype(jnp.float32)
            square += wide * wide
        mean_sq = jnp.sum(square, axis=-1, keepdims=True) / (parts * width)
        scale[...] = jnp.broadcast_to(lax.rsqrt(mean_sq + 1e-05), scale.shape)
        total[...] = jnp.zeros_like(total)
        routed[...] = jnp.zeros_like(routed)

    for k in range(each):
        part = at * each + k
        extra = rows_ref[part, slots:, :].astype(jnp.float32)
        wide = rows_ref[part, :slots, :].astype(jnp.float32)
        normed = (wide * scale[:, :1] * extra[0:1]).astype(jnp.bfloat16)
        xn_ref[:, k * width : (k + 1) * width] = normed
        routed[...] += normed.astype(jnp.float32) * extra[1:2]
        weights = in_feature_order(core, mine_ref[:, k, :64, :], other_ref[:, k, :64, :])
        total[...] += dot(normed, weights)

    @pl.when(at == steps - 1)
    def _():
        gate = jax.nn.sigmoid(jnp.sum(routed[...], axis=-1, keepdims=True))
        gate_ref[...] = jnp.broadcast_to(gate, gate_ref.shape)
        kv_ref[0] = head_norm(total[:, :head], gain_ref[...])
        live = lax.broadcasted_iota(jnp.int32, (slots, head), 0) < count
        kv_ref[1] = jnp.where(live, total[:, head:], 0.0).astype(jnp.bfloat16)


def make_keys(core, count, rows, mine, other, gain, slots):
    parts, _, width = rows.shape
    nx, _, deep, both = mine.shape
    head = gain.shape[0]
    steps = 4
    each = parts // steps
    weights = pl.BlockSpec((nx, each, deep, both), lambda i: (0, i, 0, 0))
    return pl.pallas_call(
        keys_kernel,
        grid=(steps,),
        out_shape=(
            jax.ShapeDtypeStruct((slots, parts * width), jnp.bfloat16),
            jax.ShapeDtypeStruct((2, slots, head), jnp.bfloat16),
            jax.ShapeDtypeStruct((slots, head), jnp.float32),
        ),
        in_specs=[
            whole(pltpu.SMEM),
            whole(pltpu.SMEM),
            whole(),
            weights,
            weights,
            whole(),
        ],
        out_specs=(
            pl.BlockSpec((slots, each * width), lambda i: (0, i)),
            whole(),
            whole(),
        ),
        scratch_shapes=[
            pltpu.VMEM((slots, both), jnp.float32),
            pltpu.VMEM((slots, width), jnp.float32),
            pltpu.VMEM((slots, head), jnp.float32),
        ],
        compiler_params=params(),
        name="make_keys",
    )(core, count, rows, mine, other, gain.reshape(1, head))


def queries_kernel(xn_ref, weights_ref, gain_ref, out_ref, total):
    blocks, each, deep, width = weights_ref.shape
    head = gain_ref.shape[1]
    at = pl.program_id(0)

    @pl.when(at == 0)
    def _():
        total[...] = jnp.zeros_like(total)

    for k in range(each):
        weights = weights_ref[:, k].reshape(blocks * deep, width)
        total[...] += dot(xn_ref[:, k * blocks * deep : (k + 1) * blocks * deep], weights)

    @pl.when(at == pl.num_programs(0) - 1)
    def _():
        for h in range(0, width, head):
            out_ref[:, h : h + head] = head_norm(total[:, h : h + head], gain_ref[...])


def make_queries(xn, weights, gain):
    blocks, parts, deep, width = weights.shape
    slots = xn.shape[0]
    steps = 4
    each = parts // steps
    return pl.pallas_call(
        queries_kernel,
        grid=(steps,),
        out_shape=jax.ShapeDtypeStruct((slots, width), jnp.bfloat16),
        in_specs=[
            pl.BlockSpec((slots, each * blocks * deep), lambda i: (0, i)),
            pl.BlockSpec((blocks, each, deep, width), lambda i: (0, i, 0, 0)),
            whole(),
        ],
        out_specs=whole(),
        scratch_shapes=[pltpu.VMEM((slots, width), jnp.float32)],
        compiler_params=params(),
        name="make_queries",
    )(xn, weights, gain.reshape(1, -1))


def attend_kernel(
    place_ref, lengths_ref, count_ref, q_ref, own_ref, keys_ref, mine_ref, other_ref, pos_row_ref, pos_col_ref,
    gate_ref, out_ref, packed, total, end_ref,
):
    slots, head = gate_ref.shape
    group = q_ref.shape[1] // head
    core, count = place_ref[0], count_ref[0]
    step, steps = pl.program_id(0), pl.num_programs(0)
    factor = math.log2(math.e) / math.sqrt(head)
    fill = lax.broadcasted_iota(jnp.int32, (slots, head), 0)

    @pl.when(step == 0)
    def _():
        end_ref[0] = 0
        allowed = (pos_row_ref[...] <= pos_col_ref[...]) & (
            lax.broadcasted_iota(jnp.int32, (slots, slots), 1) < count
        )
        summed = jnp.concatenate([own_ref[1], jnp.ones((slots, head), jnp.bfloat16)], axis=1)
        for h in range(group):
            query = q_ref[:, h * head : (h + 1) * head]
            weights = jnp.exp2(dot(query, own_ref[0], 1, 1) * factor)
            weights = jnp.where(allowed, weights, 0.0).astype(jnp.bfloat16)
            total[h] = dot(weights, summed)

    def pack(at, offset):
        for which, ref in enumerate((mine_ref, other_ref)):
            length = lengths_ref[which, step * mine_ref.shape[1] + at]
            side = jnp.where(core == 0, which, 1 - which)

            @pl.when(length > 0)
            def _():
                where = pl.ds(pl.multiple_of(offset, 16), slots)
                packed[where, :head] = keys_ref[0, side, at]
                packed[where, head : 2 * head] = ref[0, at]
                packed[where, 2 * head :] = jnp.where(fill < length, 1.0, 0.0).astype(jnp.bfloat16)

            offset = offset + (length + 15) // 16 * 16
        return offset

    start = end_ref[0]
    end = lax.fori_loop(0, mine_ref.shape[1], pack, start)
    end_ref[0] = end

    @pl.when(step == steps - 1)
    def _():
        rest = pl.ds(pl.multiple_of(end, 16), TILE)
        packed[rest, :] = jnp.zeros((TILE, packed.shape[1]), jnp.bfloat16)

    def tile(at, carry):
        rows = pl.ds(pl.multiple_of(at * TILE, TILE), TILE)
        keys, values = packed[rows, :head], packed[rows, head:]
        for h in range(group):
            query = q_ref[:, h * head : (h + 1) * head]
            weights = jnp.exp2(dot(query, keys, 1, 1) * factor).astype(jnp.bfloat16)
            total[h] += dot(weights, values)
        return carry

    closing = jnp.where(step == steps - 1, TILE - 1, 0)
    lax.fori_loop(start // TILE, (end + closing) // TILE, tile, 0)

    @pl.when(step == steps - 1)
    def _():
        block = out_ref.shape[0]
        live = fill < count
        pieces = []
        for h in range(group):
            sums = total[h]
            piece = gate_ref[...] * sums[:, :head] / jnp.where(live, sums[:, head:], 1.0)
            pieces.append(jnp.where(live, piece, 0.0).astype(jnp.bfloat16))
        hit = (lax.broadcasted_iota(jnp.int32, (block, slots), 0) == pos_row_ref[...]) & (
            lax.broadcasted_iota(jnp.int32, (block, slots), 1) < count
        )
        one_hot = jnp.where(hit, 1.0, 0.0).astype(jnp.bfloat16)
        out_ref[...] = dot(one_hot, jnp.concatenate(pieces, axis=1)).astype(jnp.bfloat16)


def attend(core, lengths, count, queries, own, keys, mine, other, route_pos, gate, block):
    slots, width = queries.shape
    head = gate.shape[1]
    nx, ny = mine.shape[:2]
    sources = 2 * nx * ny
    most = sources * block // 8 + 16 * sources + slots + TILE
    values = pl.BlockSpec((1, ny, slots, head), lambda i: (i, 0, 0, 0))
    return pl.pallas_call(
        attend_kernel,
        grid=(nx,),
        out_shape=jax.ShapeDtypeStruct((block, width), jnp.bfloat16),
        in_specs=[
            whole(pltpu.SMEM),
            whole(pltpu.SMEM),
            whole(pltpu.SMEM),
            whole(),
            whole(),
            pl.BlockSpec((1, 2, ny, slots, head), lambda i: (i, 0, 0, 0, 0)),
            values,
            values,
            whole(),
            whole(),
            whole(),
        ],
        out_specs=whole(),
        scratch_shapes=[
            pltpu.VMEM(((most + TILE - 1) // TILE * TILE, 3 * head), jnp.bfloat16),
            pltpu.VMEM((width // head, slots, 2 * head), jnp.float32),
            pltpu.SMEM((1,), jnp.int32),
        ],
        compiler_params=params(),
        name="attend",
    )(
        core, lengths, count, queries, own, keys, mine, other,
        route_pos.reshape(1, slots), route_pos.reshape(slots, 1), gate,
    )


def to_all(block, axes, peers):
    return lax.all_to_all(
        jnp.broadcast_to(block[None], (peers,) + block.shape), axes, 0, 0, tiled=True
    )


def swap_cores(block):
    return lax.ppermute(block, "core", [(0, 1), (1, 0)])


def local(
    tokens, x_gain, w_router, w_query, key_weight, value_weight, q_gain, key_norm_gain, route_pos, route_count
):
    ny, nx, nz = lax.axis_size("y"), lax.axis_size("x"), lax.axis_size("z")
    block = tokens.shape[0]
    slots = route_pos.shape[0]
    core = lax.axis_index("core").astype(jnp.int32)
    shard = lax.axis_index(SEQ).astype(jnp.int32)
    deep, width = w_query.shape
    head = q_gain.shape[0]

    picked = pick_rows(tokens, route_pos, x_gain, w_router)
    rows = lax.all_gather(picked, "z", axis=0, tiled=False)

    weights = jnp.concatenate([w_query, key_weight, value_weight], axis=1)
    counted = jnp.full((8, weights.shape[1]), route_count[0].astype(jnp.bfloat16))
    weights_y = lax.all_gather(jnp.concatenate([weights, counted], axis=0), "y", axis=0, tiled=False)
    kv_mine = to_all(weights_y[:, :, width:], "x", nx)
    kv_other = swap_cores(kv_mine)
    wq = lax.all_gather(weights_y[:, :deep, :width], ("x", "core"), axis=0, tiled=False)

    normed, own, gate = make_keys(core[None], route_count, rows, kv_mine, kv_other, key_norm_gain, slots)

    own_y = lax.all_gather(own.reshape(2 * slots, head), "y", axis=0, tiled=False).reshape(ny, 2, slots, head)
    keys = lax.all_gather(own_y[:, 0], ("x", "core"), axis=0, tiled=False)
    keys = keys.reshape(nx, 2, ny, slots, head)
    mine = to_all(own_y[:, 1], "x", nx)
    other = swap_cores(mine)

    queries = make_queries(normed, wq, q_gain)
    counts = jnp.stack([kv_mine[:, :, deep, 0], kv_other[:, :, deep, 0]]).astype(jnp.int32)
    across, along = jnp.arange(nx, dtype=jnp.int32)[:, None], jnp.arange(ny, dtype=jnp.int32)[None, :]
    sides = jnp.stack([core, 1 - core])[:, None, None]
    earlier = (along * nx + across)[None] * 2 + sides < shard
    lengths = jnp.where(earlier, counts, 0).reshape(2, nx * ny)
    return attend(core[None], lengths, route_count, queries, own, keys, mine, other, route_pos, gate, block)


def solution(mesh):
    grid = Mesh(mesh.devices.reshape(8, 4, 2, 8), ("y", "x", "core", "z"))
    return jax.shard_map(
        local,
        mesh=grid,
        in_specs=(
            P(SEQ, "z"), P("z"), P("z"), P(SEQ, "z"), P(SEQ, "z"), P(SEQ, "z"), P(), P(), P(SEQ), P(SEQ),
        ),
        out_specs=P(SEQ, "z"),
        check_vma=False,
    )
```

```python
import math

import jax
import jax.numpy as jnp
from jax import lax
from jax.experimental import pallas as pl
from jax.experimental.pallas import tpu as pltpu
from jax.sharding import Mesh
from jax.sharding import PartitionSpec as P

SEQ = ("yh", "yl", "x", "core")
TILE = 1024
HALF = 512


def whole(memory_space=pltpu.VMEM):
    return pl.BlockSpec(memory_space=memory_space)


def params(mebibytes):
    return pltpu.CompilerParams(vmem_limit_bytes=mebibytes * 1024 * 1024)


def dot(a, b, contract_a=1, contract_b=0):
    return lax.dot_general(
        a, b, (((contract_a,), (contract_b,)), ((), ())), preferred_element_type=jnp.float32
    )


def pick_rows_kernel(tokens_ref, pos_ref, gain_ref, router_ref, out_ref):
    slots = pos_ref.shape[1]
    rows, width = tokens_ref.shape
    hit = lax.broadcasted_iota(jnp.int32, (rows, slots), 0) == pos_ref[...]
    one_hot = jnp.where(hit, 1.0, 0.0).astype(jnp.bfloat16)
    out_ref[:slots, :] = dot(one_hot, tokens_ref[...], 0, 0).astype(jnp.bfloat16)
    at = lax.broadcasted_iota(jnp.int32, (out_ref.shape[0] - slots, width), 0)
    extra = jnp.where(at == 0, gain_ref[...].astype(jnp.float32).reshape(1, width), 0.0)
    extra = jnp.where(at == 1, router_ref[...].astype(jnp.float32).reshape(1, width), extra)
    out_ref[slots:, :] = extra.astype(jnp.bfloat16)


def pick_rows(tokens, route_pos, x_gain, w_router):
    slots = route_pos.shape[0]
    width = tokens.shape[1]
    return pl.pallas_call(
        pick_rows_kernel,
        out_shape=jax.ShapeDtypeStruct((slots + 16, width), jnp.bfloat16),
        in_specs=[whole()] * 4,
        out_specs=whole(),
        compiler_params=params(8),
        name="pick_rows",
    )(tokens, route_pos.reshape(1, slots), x_gain, w_router)


def head_norm(projected, gain):
    mean_sq = jnp.mean(projected * projected, axis=-1, keepdims=True)
    return (projected * lax.rsqrt(mean_sq + 1e-06) * gain).astype(jnp.bfloat16)


def in_feature_order(core, mine, other):
    even = jnp.where(core == 0, mine, other)
    odd = jnp.where(core == 0, other, mine)
    return jnp.stack([even, odd], axis=1).reshape(-1, mine.shape[-1])


def keys_kernel(place_ref, count_ref, rows_ref, mine_ref, other_ref, gain_ref, xn_ref, kv_ref, gate_ref):
    parts, _, width = rows_ref.shape
    slots, head = gate_ref.shape
    core, count = place_ref[0], count_ref[0]
    square = jnp.zeros((slots, width), jnp.float32)
    for part in range(parts):
        wide = rows_ref[part, :slots, :].astype(jnp.float32)
        square += wide * wide
    mean_sq = jnp.sum(square, axis=-1, keepdims=True) / (parts * width)
    scale = lax.rsqrt(mean_sq + 1e-05)
    total = jnp.zeros((slots, 2 * head), jnp.float32)
    routed = jnp.zeros((slots, width), jnp.float32)
    for part in range(parts):
        extra = rows_ref[part, slots:, :].astype(jnp.float32)
        wide = rows_ref[part, :slots, :].astype(jnp.float32)
        normed = (wide * scale * extra[0:1]).astype(jnp.bfloat16)
        xn_ref[:, part * width : (part + 1) * width] = normed
        routed += normed.astype(jnp.float32) * extra[1:2]
        weights = in_feature_order(core, mine_ref[:, part], other_ref[:, part])
        total += dot(normed, weights)
    gate = jax.nn.sigmoid(jnp.sum(routed, axis=-1, keepdims=True))
    gate_ref[...] = jnp.broadcast_to(gate, gate_ref.shape)
    kv_ref[0] = head_norm(total[:, :head], gain_ref[...])
    live = lax.broadcasted_iota(jnp.int32, (slots, head), 0) < count
    kv_ref[1] = jnp.where(live, total[:, head:], 0.0).astype(jnp.bfloat16)


def make_keys(place, count, rows, mine, other, gain, slots):
    parts, _, width = rows.shape
    head = gain.shape[0]
    return pl.pallas_call(
        keys_kernel,
        out_shape=(
            jax.ShapeDtypeStruct((slots, parts * width), jnp.bfloat16),
            jax.ShapeDtypeStruct((2, slots, head), jnp.bfloat16),
            jax.ShapeDtypeStruct((slots, head), jnp.float32),
        ),
        in_specs=[whole(pltpu.SMEM)] * 2 + [whole()] * 4,
        out_specs=(whole(),) * 3,
        compiler_params=params(16),
        name="make_keys",
    )(place, count, rows, mine, other, gain.reshape(1, head))


def queries_kernel(xn_ref, weights_ref, gain_ref, out_ref, counts_ref, total):
    blocks, each, _, width = weights_ref.shape
    head = gain_ref.shape[1]
    deep = xn_ref.shape[1] // (blocks * each)
    at = pl.program_id(0)

    @pl.when(at == 0)
    def _():
        total[...] = jnp.zeros_like(total)

    for k in range(each):
        weights = weights_ref[:, k, :deep].reshape(blocks * deep, width)
        total[...] += dot(xn_ref[:, k * blocks * deep : (k + 1) * blocks * deep], weights)
        counts = jnp.max(weights_ref[:, k, deep:, :head].astype(jnp.float32), axis=1)
        counts_ref[at * each + k] = counts.astype(jnp.int32)

    @pl.when(at == pl.num_programs(0) - 1)
    def _():
        for h in range(0, width, head):
            out_ref[:, h : h + head] = head_norm(total[:, h : h + head], gain_ref[...])


def make_queries(xn, weights, gain):
    blocks, parts, padded, width = weights.shape
    slots = xn.shape[0]
    head = gain.shape[0]
    steps = 4
    each = parts // steps
    return pl.pallas_call(
        queries_kernel,
        grid=(steps,),
        out_shape=(
            jax.ShapeDtypeStruct((slots, width), jnp.bfloat16),
            jax.ShapeDtypeStruct((parts, blocks, head), jnp.int32),
        ),
        in_specs=[
            pl.BlockSpec((slots, xn.shape[1] // steps), lambda i: (0, i)),
            pl.BlockSpec((blocks, each, padded, width), lambda i: (0, i, 0, 0)),
            whole(),
        ],
        out_specs=(whole(), whole()),
        scratch_shapes=[pltpu.VMEM((slots, width), jnp.float32)],
        compiler_params=params(16),
        name="make_queries",
    )(xn, weights, gain.reshape(1, -1))


def pack(place_ref, counts_ref, nx, store):
    ny = counts_ref.shape[0]
    core, shard = place_ref[0], place_ref[1]

    def step(at, offset):
        x, y = at // ny, at % ny
        for which in range(2):
            side = jnp.where(core == 0, which, 1 - which)
            earlier = (y * nx + x) * 2 + side < shard
            length = jnp.where(earlier, counts_ref[y, x * 2 + side, 0], 0)

            @pl.when(length > 0)
            def _():
                store(pl.multiple_of(offset, 16), which, side, x, y, length)

            offset = offset + (length + 15) // 16 * 16
        return offset

    return lax.fori_loop(0, nx * ny, step, jnp.int32(0))


def scores_kernel(
    place_ref, counts_ref, count_ref, q_ref, own_ref, mine_ref, other_ref, pos_row_ref, pos_col_ref,
    out_ref, sums_ref, packed, end_ref,
):
    slots, head = own_ref.shape[1:]
    group = q_ref.shape[1] // head
    count = count_ref[0]
    at = pl.program_id(0)
    factor = math.log2(math.e) / math.sqrt(head)

    @pl.when(at == 0)
    def _():
        def store(offset, which, side, x, y, length):
            packed[pl.ds(offset, slots), :] = (mine_ref, other_ref)[which][x, y]

        end = pack(place_ref, counts_ref, mine_ref.shape[0], store)
        end_ref[0] = end
        packed[pl.ds(pl.multiple_of(end, 16), TILE), :] = jnp.zeros((TILE, head), jnp.bfloat16)
        allowed = (pos_row_ref[...] <= pos_col_ref[...]) & (
            lax.broadcasted_iota(jnp.int32, (slots, slots), 1) < count
        )
        summed = jnp.concatenate([own_ref[1], jnp.ones((slots, head), jnp.bfloat16)], axis=1)
        for h in range(group):
            query = q_ref[:, h * head : (h + 1) * head]
            weights = jnp.exp2(dot(query, own_ref[0], 1, 1) * factor)
            weights = jnp.where(allowed, weights, 0.0).astype(jnp.bfloat16)
            sums_ref[h] = dot(weights, summed)

    for half in range(0, TILE, HALF):

        @pl.when(at * TILE + half < end_ref[0])
        def _():
            keys = packed[pl.ds(pl.multiple_of(at * TILE + half, HALF), HALF), :]
            for h in range(group):
                query = q_ref[:, h * head : (h + 1) * head]
                weights = jnp.exp2(dot(query, keys, 1, 1) * factor)
                out_ref[h, :, half : half + HALF] = weights.astype(jnp.bfloat16)


def packed_rows(sources, block, slots):
    return -(-(sources * block // 8 + 16 * sources) // TILE) * TILE


def scores(place, counts, count, queries, own, mine, other, route_pos, block):
    slots, width = queries.shape
    head = own.shape[2]
    nx, ny = mine.shape[:2]
    rows = packed_rows(2 * nx * ny, block, slots)
    group = width // head
    return pl.pallas_call(
        scores_kernel,
        grid=(rows // TILE,),
        out_shape=(
            jax.ShapeDtypeStruct((group, slots, rows), jnp.bfloat16),
            jax.ShapeDtypeStruct((group, slots, 2 * head), jnp.float32),
        ),
        in_specs=[whole(pltpu.SMEM)] * 3 + [whole()] * 6,
        out_specs=(pl.BlockSpec((group, slots, TILE), lambda i: (0, 0, i)), whole()),
        scratch_shapes=[pltpu.VMEM((rows + TILE, head), jnp.bfloat16), pltpu.SMEM((1,), jnp.int32)],
        compiler_params=params(24),
        name="scores",
    )(place, counts, count, queries, own, mine, other, route_pos.reshape(1, slots), route_pos.reshape(slots, 1))


def attend_kernel(
    place_ref, counts_ref, count_ref, weights_ref, sums_ref, values_ref, pos_row_ref, gate_ref,
    out_ref, packed, total, end_ref,
):
    slots, head = gate_ref.shape
    group = weights_ref.shape[0]
    count = count_ref[0]
    at = pl.program_id(0)
    fill = lax.broadcasted_iota(jnp.int32, (slots, head), 0)

    @pl.when(at == 0)
    def _():
        def store(offset, which, side, x, y, length):
            packed[pl.ds(offset, slots), :head] = values_ref[x, side, y]
            packed[pl.ds(offset, slots), head:] = jnp.where(fill < length, 1.0, 0.0).astype(jnp.bfloat16)

        end = pack(place_ref, counts_ref, values_ref.shape[0], store)
        end_ref[0] = end
        packed[pl.ds(pl.multiple_of(end, 16), TILE), :] = jnp.zeros((TILE, 2 * head), jnp.bfloat16)
        total[...] = sums_ref[...]

    for half in range(0, TILE, HALF):

        @pl.when(at * TILE + half < end_ref[0])
        def _():
            values = packed[pl.ds(pl.multiple_of(at * TILE + half, HALF), HALF), :]
            for h in range(group):
                total[h] += dot(weights_ref[h, :, half : half + HALF], values)

    @pl.when(at == pl.num_programs(0) - 1)
    def _():
        block = out_ref.shape[0]
        live = fill < count
        pieces = []
        for h in range(group):
            sums = total[h]
            piece = gate_ref[...] * sums[:, :head] / jnp.where(live, sums[:, head:], 1.0)
            pieces.append(jnp.where(live, piece, 0.0).astype(jnp.bfloat16))
        hit = (lax.broadcasted_iota(jnp.int32, (block, slots), 0) == pos_row_ref[...]) & (
            lax.broadcasted_iota(jnp.int32, (block, slots), 1) < count
        )
        one_hot = jnp.where(hit, 1.0, 0.0).astype(jnp.bfloat16)
        out_ref[...] = dot(one_hot, jnp.concatenate(pieces, axis=1)).astype(jnp.bfloat16)


def attend(place, counts, count, weights, sums, values, route_pos, gate, block):
    group, slots, rows = weights.shape
    head = gate.shape[1]
    return pl.pallas_call(
        attend_kernel,
        grid=(rows // TILE,),
        out_shape=jax.ShapeDtypeStruct((block, group * head), jnp.bfloat16),
        in_specs=[whole(pltpu.SMEM)] * 3
        + [pl.BlockSpec((group, slots, TILE), lambda i: (0, 0, i))]
        + [whole()] * 4,
        out_specs=whole(),
        scratch_shapes=[
            pltpu.VMEM((rows + TILE, 2 * head), jnp.bfloat16),
            pltpu.VMEM((group, slots, 2 * head), jnp.float32),
            pltpu.SMEM((1,), jnp.int32),
        ],
        compiler_params=params(24),
        name="attend",
    )(place, counts, count, weights, sums, values, route_pos.reshape(1, slots), gate)


def to_all(block, axes, peers):
    return lax.all_to_all(
        jnp.broadcast_to(block[None], (peers,) + block.shape), axes, 0, 0, tiled=True
    )


def over_y(block):
    pair = lax.all_gather(block, "yl", axis=0, tiled=False)
    every = lax.all_gather(pair, "yh", axis=0, tiled=False)
    return every.reshape((-1,) + block.shape)


def swap_cores(block):
    return lax.ppermute(block, "core", [(0, 1), (1, 0)])


def local(
    tokens, x_gain, w_router, w_query, key_weight, value_weight, q_gain, key_norm_gain, route_pos, route_count
):
    ny, nx = lax.axis_size(("yh", "yl")), lax.axis_size("x")
    block = tokens.shape[0]
    slots = route_pos.shape[0]
    place = jnp.stack([lax.axis_index("core"), lax.axis_index(SEQ)]).astype(jnp.int32)
    deep, width = w_query.shape
    head = q_gain.shape[0]

    picked = pick_rows(tokens, route_pos, x_gain, w_router)
    rows = lax.all_gather(picked, "z", axis=0, tiled=False)

    weights = jnp.concatenate([w_query, key_weight, value_weight], axis=1)
    counted = jnp.full((16, weights.shape[1]), route_count[0].astype(jnp.bfloat16))
    weights_y = over_y(jnp.concatenate([weights, counted], axis=0))
    kv_mine = to_all(weights_y[:, :deep, width:], "x", nx)
    weights_y, kv_mine = lax.optimization_barrier((weights_y, kv_mine))
    kv_other = swap_cores(kv_mine)
    wq = lax.all_gather(weights_y[:, :, :width], ("x", "core"), axis=0, tiled=False)

    normed, own, gate = make_keys(place, route_count, rows, kv_mine, kv_other, key_norm_gain, slots)

    own_y = over_y(own.reshape(2 * slots, head)).reshape(ny, 2, slots, head)
    values = lax.all_gather(own_y[:, 1], ("x", "core"), axis=0, tiled=False).reshape(nx, 2, ny, slots, head)
    mine = to_all(own_y[:, 0], "x", nx)
    other = swap_cores(mine)

    queries, counts = make_queries(normed, wq, q_gain)
    parts, sums = scores(place, counts, route_count, queries, own, mine, other, route_pos, block)
    return attend(place, counts, route_count, parts, sums, values, route_pos, gate, block)


def solution(mesh):
    grid = Mesh(mesh.devices.reshape(4, 2, 4, 2, 8), SEQ + ("z",))
    return jax.shard_map(
        local,
        mesh=grid,
        in_specs=(
            P(SEQ, "z"), P("z"), P("z"), P(SEQ, "z"), P(SEQ, "z"), P(SEQ, "z"), P(), P(), P(SEQ), P(SEQ),
        ),
        out_specs=P(SEQ, "z"),
        check_vma=False,
    )
```

```python
import math

import jax
import jax.numpy as jnp
from jax import lax
from jax.experimental import pallas as pl
from jax.experimental.pallas import tpu as pltpu
from jax.sharding import Mesh
from jax.sharding import PartitionSpec as P

SEQ = ("y", "x", "core")
TILE = 1024
HALF = 512


def whole(memory_space=pltpu.VMEM):
    return pl.BlockSpec(memory_space=memory_space)


def params(mebibytes=56):
    return pltpu.CompilerParams(vmem_limit_bytes=mebibytes * 1024 * 1024)


def dot(a, b, contract_a=1, contract_b=0):
    return lax.dot_general(
        a, b, (((contract_a,), (contract_b,)), ((), ())), preferred_element_type=jnp.float32
    )


def stage_kernel(
    count_ref, tokens_ref, pos_ref, gain_ref, router_ref, query_ref, key_ref, value_ref, rows_ref, weights_ref
):
    slots = pos_ref.shape[1]
    block, width = tokens_ref.shape
    hit = lax.broadcasted_iota(jnp.int32, (block, slots), 0) == pos_ref[...]
    one_hot = jnp.where(hit, 1.0, 0.0).astype(jnp.bfloat16)
    rows_ref[:slots, :] = dot(one_hot, tokens_ref[...], 0, 0).astype(jnp.bfloat16)
    at = lax.broadcasted_iota(jnp.int32, (rows_ref.shape[0] - slots, width), 0)
    extra = jnp.where(at == 0, gain_ref[...].astype(jnp.float32).reshape(1, width), 0.0)
    extra = jnp.where(at == 1, router_ref[...].astype(jnp.float32).reshape(1, width), extra)
    rows_ref[slots:, :] = extra.astype(jnp.bfloat16)
    deep, query = query_ref.shape
    key = key_ref.shape[1]
    weights_ref[:deep, :query] = query_ref[...]
    weights_ref[:deep, query : query + key] = key_ref[...]
    weights_ref[:deep, query + key :] = value_ref[...]
    count = jnp.full((weights_ref.shape[0] - deep, weights_ref.shape[1]), count_ref[0], jnp.int32)
    weights_ref[deep:, :] = count.astype(jnp.float32).astype(jnp.bfloat16)


def stage(count, tokens, route_pos, x_gain, w_router, w_query, key_weight, value_weight):
    slots = route_pos.shape[0]
    width = tokens.shape[1]
    deep = w_query.shape[0]
    across = w_query.shape[1] + key_weight.shape[1] + value_weight.shape[1]
    return pl.pallas_call(
        stage_kernel,
        out_shape=(
            jax.ShapeDtypeStruct((slots + 16, width), jnp.bfloat16),
            jax.ShapeDtypeStruct((deep + 8, across), jnp.bfloat16),
        ),
        in_specs=[whole(pltpu.SMEM)] + [whole()] * 7,
        out_specs=(whole(), whole()),
        compiler_params=params(),
        name="stage",
    )(count, tokens, route_pos.reshape(1, slots), x_gain, w_router, w_query, key_weight, value_weight)


def head_norm(projected, gain):
    mean_sq = jnp.mean(projected * projected, axis=-1, keepdims=True)
    return (projected * lax.rsqrt(mean_sq + 1e-06) * gain).astype(jnp.bfloat16)


def in_feature_order(core, mine, other):
    even = jnp.where(core == 0, mine, other)
    odd = jnp.where(core == 0, other, mine)
    return jnp.stack([even, odd], axis=1).reshape(-1, mine.shape[-1])


def norm_scale(rows_ref, slots):
    parts, _, width = rows_ref.shape
    square = jnp.zeros((slots, width), jnp.float32)
    for part in range(parts):
        wide = rows_ref[part, :slots, :].astype(jnp.float32)
        square += wide * wide
    mean_sq = jnp.sum(square, axis=-1, keepdims=True) / (parts * width)
    return lax.rsqrt(mean_sq + 1e-05)


def normed_part(rows_ref, part, slots, scale):
    extra = rows_ref[part, slots:, :].astype(jnp.float32)
    wide = rows_ref[part, :slots, :].astype(jnp.float32)
    return (wide * scale * extra[0:1]).astype(jnp.bfloat16), extra[1:2]


def keys_kernel(place_ref, count_ref, rows_ref, mine_ref, other_ref, gain_ref, kv_ref, counts_ref):
    slots, head = kv_ref.shape[1:]
    nx, parts, _, both = mine_ref.shape
    deep = rows_ref.shape[2] // (2 * nx)
    core, count = place_ref[0], count_ref[0]
    scale = norm_scale(rows_ref, slots)
    total = jnp.zeros((slots, both), jnp.float32)
    for part in range(parts):
        block, _ = normed_part(rows_ref, part, slots, scale)
        weights = in_feature_order(core, mine_ref[:, part, :deep], other_ref[:, part, :deep])
        total += dot(block, weights)
    kv_ref[0] = head_norm(total[:, :head], gain_ref[...])
    live = lax.broadcasted_iota(jnp.int32, (slots, head), 0) < count
    kv_ref[1] = jnp.where(live, total[:, head:], 0.0).astype(jnp.bfloat16)
    for which, ref in enumerate((mine_ref, other_ref)):
        for x in range(nx):
            counts = jnp.max(ref[x, :, deep:, :head].astype(jnp.float32), axis=1)
            counts_ref[which, x] = counts.astype(jnp.int32)


def make_keys(place, count, rows, mine, other, gain, slots):
    nx, ny = mine.shape[:2]
    head = gain.shape[0]
    return pl.pallas_call(
        keys_kernel,
        out_shape=(
            jax.ShapeDtypeStruct((2, slots, head), jnp.bfloat16),
            jax.ShapeDtypeStruct((2, nx, ny, head), jnp.int32),
        ),
        in_specs=[whole(pltpu.SMEM)] * 2 + [whole()] * 4,
        out_specs=(whole(), whole()),
        compiler_params=params(16),
        name="make_keys",
    )(place, count, rows, mine, other, gain.reshape(1, head))


def queries_kernel(
    place_ref, rows_hbm, mine_hbm, other_hbm, gain_ref, out_ref, gate_ref, rows, weights, rows_here, weights_here
):
    parts, nx, _, deep, width = weights.shape
    slots, head = gate_ref.shape
    core = place_ref[0]
    rows_copies, weights_copies = [], []
    for part in range(parts):
        rows_copies.append(pltpu.make_async_copy(rows_hbm.at[part], rows.at[part], rows_here.at[part]))
        rows_copies[part].start()
    for part in range(parts):
        weights_copies.append(
            [
                pltpu.make_async_copy(source.at[:, part], weights.at[part, :, side], weights_here.at[which, part])
                for which, (source, side) in enumerate(((mine_hbm, core), (other_hbm, 1 - core)))
            ]
        )
        for copy in weights_copies[part]:
            copy.start()
    for copy in rows_copies:
        copy.wait()
    scale = norm_scale(rows, slots)
    routed = jnp.zeros((slots, rows.shape[2]), jnp.float32)
    total = jnp.zeros((slots, width), jnp.float32)
    for part in range(parts):
        block, router = normed_part(rows, part, slots, scale)
        routed += block.astype(jnp.float32) * router
        for copy in weights_copies[part]:
            copy.wait()
        total += dot(block, weights[part].reshape(nx * 2 * deep, width))
    gate = jax.nn.sigmoid(jnp.sum(routed, axis=-1, keepdims=True))
    gate_ref[...] = jnp.broadcast_to(gate, gate_ref.shape)
    for h in range(0, width, head):
        out_ref[:, h : h + head] = head_norm(total[:, h : h + head], gain_ref[...])


def make_queries(place, rows, mine, other, gain, slots):
    nx, parts, deep, width = mine.shape
    head = gain.shape[0]
    return pl.pallas_call(
        queries_kernel,
        out_shape=(
            jax.ShapeDtypeStruct((slots, width), jnp.bfloat16),
            jax.ShapeDtypeStruct((slots, head), jnp.float32),
        ),
        in_specs=[whole(pltpu.SMEM)] + [whole(pl.ANY)] * 3 + [whole()],
        out_specs=(whole(), whole()),
        scratch_shapes=[
            pltpu.VMEM(rows.shape, jnp.bfloat16),
            pltpu.VMEM((parts, nx, 2, deep, width), jnp.bfloat16),
            pltpu.SemaphoreType.DMA((parts,)),
            pltpu.SemaphoreType.DMA((2, parts)),
        ],
        compiler_params=params(),
        name="make_queries",
    )(place, rows, mine, other, gain.reshape(1, -1))


def pack_kernel(
    place_ref, counts_ref, count_ref, mine_hbm, other_hbm, _, keys_ref, flags, table_ref, mine_ref, other_ref, here
):
    nx, ny, slots, head = mine_ref.shape
    copies = [
        [
            pltpu.make_async_copy(source.at[x], target.at[x], here.at[which, x])
            for which, (source, target) in enumerate(((mine_hbm, mine_ref), (other_hbm, other_ref)))
        ]
        for x in range(nx)
    ]
    for pair in copies:
        for copy in pair:
            copy.start()
    core, shard = place_ref[0], place_ref[1]
    fill = lax.broadcasted_iota(jnp.int32, (slots, head), 0)

    end = jnp.int32(0)
    for x in range(nx):
        for copy in copies[x]:
            copy.wait()
        for y in range(ny):
            for which, ref in enumerate((mine_ref, other_ref)):
                side = jnp.where(core == 0, which, 1 - which)
                earlier = (y * nx + x) * 2 + side < shard
                length = jnp.where(earlier, counts_ref[which, x, y, 0], 0)
                table_ref[which, x * ny + y] = jnp.where(length > 0, end, -1)

                @pl.when(length > 0)
                def _():
                    where = pl.ds(pl.multiple_of(end, 16), slots)
                    keys_ref[where, :] = ref[x, y]
                    flags[where, :] = jnp.where(fill < length, 1.0, 0.0).astype(jnp.bfloat16)

                end = end + (length + 15) // 16 * 16
        table_ref[2, 3 + x] = end
    table_ref[2, 0] = end
    table_ref[2, 1] = core
    table_ref[2, 2] = count_ref[0]
    rest = pl.ds(pl.multiple_of(end, 16), TILE)
    keys_ref[rest, :] = jnp.zeros((TILE, head), jnp.bfloat16)
    flags[rest, :] = jnp.zeros((TILE, head), jnp.bfloat16)


def packed_rows(sources, block):
    return -(-(sources * block // 8 + 16 * sources) // TILE) * TILE


def pack_keys(place, counts, count, mine, other, after, block):
    nx, ny, _, head = mine.shape
    rows = packed_rows(2 * nx * ny, block)
    return pl.pallas_call(
        pack_kernel,
        out_shape=(
            jax.ShapeDtypeStruct((rows + TILE, head), jnp.bfloat16),
            jax.ShapeDtypeStruct((rows + TILE, head), jnp.bfloat16),
            jax.ShapeDtypeStruct((3, nx * ny), jnp.int32),
        ),
        in_specs=[whole(pltpu.SMEM)] * 3 + [whole(pl.ANY)] * 3,
        out_specs=(whole(), whole(), whole(pltpu.SMEM)),
        scratch_shapes=[
            pltpu.VMEM(mine.shape, jnp.bfloat16),
            pltpu.VMEM(other.shape, jnp.bfloat16),
            pltpu.SemaphoreType.DMA((2, nx)),
        ],
        compiler_params=params(),
        name="pack_keys",
    )(place, counts, count, mine, other, after)


def attend_kernel(
    table_ref, q_ref, own_ref, pos_row_ref, gate_ref, keys_hbm, flags_hbm, values_hbm,
    out_ref, keys_ref, values, packed, total, arrived, chunks,
):
    nx, _, ny, slots, head = values.shape
    group = q_ref.shape[1] // head
    end, core, count = table_ref[2, 0], table_ref[2, 1], table_ref[2, 2]
    factor = math.log2(math.e) / math.sqrt(head)
    copies = [pltpu.make_async_copy(values_hbm.at[x], values.at[x], arrived.at[x]) for x in range(nx)]
    halves = (end + HALF - 1) // HALF

    def chunk(at):
        rows = pl.ds(pl.multiple_of(at * TILE, TILE), TILE)
        return (
            pltpu.make_async_copy(keys_hbm.at[rows, :], keys_ref.at[rows, :], chunks.at[0, at]),
            pltpu.make_async_copy(flags_hbm.at[rows, :], packed.at[rows, head:], chunks.at[1, at]),
        )

    def begin(at, carry):
        for copy in chunk(at):
            copy.start()
        return carry

    copies[0].start()
    lax.fori_loop(0, (halves + 1) // 2, begin, 0)
    for copy in copies[1:]:
        copy.start()

    across = lax.broadcasted_iota(jnp.int32, (slots, slots), 1)
    along = lax.broadcasted_iota(jnp.int32, (slots, slots), 0)
    positions = jnp.broadcast_to(pos_row_ref[...].astype(jnp.float32), (slots, slots))
    mine = jnp.sum(jnp.where(across == along, positions, 0.0), axis=1, keepdims=True)
    allowed = (positions <= mine) & (across < count)
    summed = jnp.concatenate([own_ref[1], jnp.ones((slots, head), jnp.bfloat16)], axis=1)
    for h in range(group):
        query = q_ref[:, h * head : (h + 1) * head]
        weights = jnp.exp2(dot(query, own_ref[0], 1, 1) * factor)
        total[h] = dot(jnp.where(allowed, weights, 0.0).astype(jnp.bfloat16), summed)

    def weigh(start, size):
        rows = pl.ds(pl.multiple_of(start, size), size)
        keys, vals = keys_ref[rows, :], packed[rows, :]
        for h in range(group):
            query = q_ref[:, h * head : (h + 1) * head]
            weights = jnp.exp2(dot(query, keys, 1, 1) * factor).astype(jnp.bfloat16)
            total[h] += dot(weights, vals)

    def tile(at, carry):
        for copy in chunk(at):
            copy.wait()
        weigh(at * TILE, TILE)
        return carry

    done = jnp.int32(0)
    for x in range(nx):
        copies[x].wait()
        for y in range(ny):
            for which in range(2):
                offset = table_ref[which, x * ny + y]

                @pl.when(offset >= 0)
                def _():
                    side = jnp.where(core == 0, which, 1 - which)
                    packed[pl.ds(pl.multiple_of(offset, 16), slots), :head] = values[x, side, y]

        if x == nx - 1:
            packed[pl.ds(pl.multiple_of(end, 16), TILE), :head] = jnp.zeros((TILE, head), jnp.bfloat16)
        ready = halves // 2 if x == nx - 1 else table_ref[2, 3 + x] // TILE
        lax.fori_loop(done, ready, tile, 0)
        done = ready

    @pl.when(halves % 2 == 1)
    def _():
        for copy in chunk(done):
            copy.wait()
        weigh(done * TILE, HALF)

    block = out_ref.shape[0]
    live = lax.broadcasted_iota(jnp.int32, (slots, 1), 0) < count
    pieces = []
    for h in range(group):
        sums = total[h]
        scale = jnp.where(live, gate_ref[...] / jnp.where(live, sums[:, head:], 1.0), 0.0)
        pieces.append((sums[:, :head] * scale).astype(jnp.bfloat16))
    hit = (lax.broadcasted_iota(jnp.int32, (block, slots), 0) == pos_row_ref[...]) & (
        lax.broadcasted_iota(jnp.int32, (block, slots), 1) < count
    )
    one_hot = jnp.where(hit, 1.0, 0.0).astype(jnp.bfloat16)
    out_ref[...] = dot(one_hot, jnp.concatenate(pieces, axis=1)).astype(jnp.bfloat16)


def attend(table, queries, own, keys, flags, route_pos, gate, values, block):
    slots, width = queries.shape
    head = gate.shape[1]
    group = width // head
    return pl.pallas_call(
        attend_kernel,
        out_shape=jax.ShapeDtypeStruct((block, width), jnp.bfloat16),
        in_specs=[whole(pltpu.SMEM)] + [whole()] * 4 + [whole(pltpu.HBM)] * 3,
        out_specs=whole(),
        scratch_shapes=[
            pltpu.VMEM(keys.shape, jnp.bfloat16),
            pltpu.VMEM(values.shape, jnp.bfloat16),
            pltpu.VMEM((keys.shape[0], 2 * head), jnp.bfloat16),
            pltpu.VMEM((group, slots, 2 * head), jnp.float32),
            pltpu.SemaphoreType.DMA((values.shape[0],)),
            pltpu.SemaphoreType.DMA((2, keys.shape[0] // TILE)),
        ],
        compiler_params=params(),
        name="attend",
    )(table, queries, own, route_pos.reshape(1, slots), gate, keys, flags, values)


def to_all(block, axes, peers):
    return lax.all_to_all(
        jnp.broadcast_to(block[None], (peers,) + block.shape), axes, 0, 0, tiled=True
    )


def swap_cores(block):
    return lax.ppermute(block, "core", [(0, 1), (1, 0)])


def local(
    tokens, x_gain, w_router, w_query, key_weight, value_weight, q_gain, key_norm_gain, route_pos, route_count
):
    ny, nx = lax.axis_size("y"), lax.axis_size("x")
    block = tokens.shape[0]
    slots = route_pos.shape[0]
    place = jnp.stack([lax.axis_index("core"), lax.axis_index(SEQ)]).astype(jnp.int32)
    deep, width = w_query.shape
    head = q_gain.shape[0]

    picked, weights = stage(
        route_count, tokens, route_pos, x_gain, w_router, w_query, key_weight, value_weight
    )
    rows = lax.all_gather(picked, "z", axis=0, tiled=False)

    weights_y = lax.all_gather(weights, "y", axis=0, tiled=False)
    kv_mine = to_all(weights_y[:, :, width:], "x", nx)
    kv_other = swap_cores(kv_mine)
    wq_mine = lax.all_gather(weights_y[:, :deep, :width], "x", axis=0, tiled=False)
    wq_other = swap_cores(wq_mine)

    own, counts = make_keys(place, route_count, rows, kv_mine, kv_other, key_norm_gain, slots)

    own_y = lax.all_gather(own.reshape(2 * slots, head), "y", axis=0, tiled=False)
    own_y = own_y.reshape(ny, 2, slots, head)
    values = lax.all_gather(own_y[:, 1], ("x", "core"), axis=0, tiled=False).reshape(nx, 2, ny, slots, head)
    mine = to_all(own_y[:, 0], "x", nx)
    other = swap_cores(mine)

    queries, gate = make_queries(place, rows, wq_mine, wq_other, q_gain, slots)
    keys, flags, table = pack_keys(place, counts, route_count, mine, other, queries, block)
    return attend(table, queries, own, keys, flags, route_pos, gate, values, block)


def solution(mesh):
    grid = Mesh(mesh.devices.reshape(8, 4, 2, 8), SEQ + ("z",))
    return jax.shard_map(
        local,
        mesh=grid,
        in_specs=(
            P(SEQ, "z"), P("z"), P("z"), P(SEQ, "z"), P(SEQ, "z"), P(SEQ, "z"), P(), P(), P(SEQ), P(SEQ),
        ),
        out_specs=P(SEQ, "z"),
        check_vma=False,
    )
```

```python
import math

import jax
import jax.numpy as jnp
from jax import lax
from jax.experimental import pallas as pl
from jax.experimental.pallas import tpu as pltpu
from jax.sharding import Mesh
from jax.sharding import PartitionSpec as P

SEQ = ("y", "x", "core")
TILE = 1024
PIECE = 256


def whole(memory_space=pltpu.VMEM):
    return pl.BlockSpec(memory_space=memory_space)


def params(mebibytes=56):
    return pltpu.CompilerParams(vmem_limit_bytes=mebibytes * 1024 * 1024)


def dot(a, b, contract_a=1, contract_b=0):
    return lax.dot_general(
        a, b, (((contract_a,), (contract_b,)), ((), ())), preferred_element_type=jnp.float32
    )


def stage_kernel(
    count_ref, tokens_ref, pos_ref, gain_ref, router_ref, query_ref, key_ref, value_ref, rows_ref, weights_ref
):
    slots = pos_ref.shape[1]
    block, width = tokens_ref.shape
    hit = lax.broadcasted_iota(jnp.int32, (block, slots), 0) == pos_ref[...]
    one_hot = jnp.where(hit, 1.0, 0.0).astype(jnp.bfloat16)
    rows_ref[:slots, :] = dot(one_hot, tokens_ref[...], 0, 0).astype(jnp.bfloat16)
    at = lax.broadcasted_iota(jnp.int32, (rows_ref.shape[0] - slots, width), 0)
    extra = jnp.where(at == 0, gain_ref[...].astype(jnp.float32).reshape(1, width), 0.0)
    extra = jnp.where(at == 1, router_ref[...].astype(jnp.float32).reshape(1, width), extra)
    rows_ref[slots:, :] = extra.astype(jnp.bfloat16)
    deep, query = query_ref.shape
    key = key_ref.shape[1]
    weights_ref[:deep, :query] = query_ref[...]
    weights_ref[:deep, query : query + key] = key_ref[...]
    weights_ref[:deep, query + key :] = value_ref[...]
    count = jnp.full((weights_ref.shape[0] - deep, weights_ref.shape[1]), count_ref[0], jnp.int32)
    weights_ref[deep:, :] = count.astype(jnp.float32).astype(jnp.bfloat16)


def stage(count, tokens, route_pos, x_gain, w_router, w_query, key_weight, value_weight):
    slots = route_pos.shape[0]
    width = tokens.shape[1]
    deep = w_query.shape[0]
    across = w_query.shape[1] + key_weight.shape[1] + value_weight.shape[1]
    return pl.pallas_call(
        stage_kernel,
        out_shape=(
            jax.ShapeDtypeStruct((slots + 8, width), jnp.bfloat16),
            jax.ShapeDtypeStruct((deep + 8, across), jnp.bfloat16),
        ),
        in_specs=[whole(pltpu.SMEM)] + [whole()] * 7,
        out_specs=(whole(), whole()),
        compiler_params=params(),
        name="stage",
    )(count, tokens, route_pos.reshape(1, slots), x_gain, w_router, w_query, key_weight, value_weight)


def head_norm(projected, gain):
    mean_sq = jnp.mean(projected * projected, axis=-1, keepdims=True)
    return (projected * lax.rsqrt(mean_sq + 1e-06) * gain).astype(jnp.bfloat16)


def in_feature_order(core, mine, other):
    even = jnp.where(core == 0, mine, other)
    odd = jnp.where(core == 0, other, mine)
    return jnp.stack([even, odd], axis=1).reshape(-1, mine.shape[-1])


def norm_scale(rows_ref, slots):
    parts, _, width = rows_ref.shape
    square = jnp.zeros((slots, width), jnp.float32)
    for part in range(parts):
        wide = rows_ref[part, :slots, :].astype(jnp.float32)
        square += wide * wide
    mean_sq = jnp.sum(square, axis=-1, keepdims=True) / (parts * width)
    return lax.rsqrt(mean_sq + 1e-05)


def normed_part(rows_ref, part, slots, scale):
    extra = rows_ref[part, slots:, :].astype(jnp.float32)
    wide = rows_ref[part, :slots, :].astype(jnp.float32)
    return (wide * scale * extra[0:1]).astype(jnp.bfloat16), extra[1:2]


def keys_kernel(place_ref, count_ref, rows_ref, mine_ref, other_ref, gain_ref, kv_ref, counts_ref):
    slots, head = kv_ref.shape[1:]
    nx, parts, _, both = mine_ref.shape
    deep = rows_ref.shape[2] // (2 * nx)
    core, count = place_ref[0], count_ref[0]
    scale = norm_scale(rows_ref, slots)
    total = jnp.zeros((slots, both), jnp.float32)
    for part in range(parts):
        block, _ = normed_part(rows_ref, part, slots, scale)
        weights = in_feature_order(core, mine_ref[:, part, :deep], other_ref[:, part, :deep])
        total += dot(block, weights)
    kv_ref[0] = head_norm(total[:, :head], gain_ref[...])
    live = lax.broadcasted_iota(jnp.int32, (slots, head), 0) < count
    kv_ref[1] = jnp.where(live, total[:, head:], 0.0).astype(jnp.bfloat16)
    for which, ref in enumerate((mine_ref, other_ref)):
        for x in range(nx):
            counts = jnp.max(ref[x, :, deep:, :head].astype(jnp.float32), axis=1)
            counts_ref[which, x] = counts.astype(jnp.int32)


def make_keys(place, count, rows, mine, other, gain, slots):
    nx, ny = mine.shape[:2]
    head = gain.shape[0]
    return pl.pallas_call(
        keys_kernel,
        out_shape=(
            jax.ShapeDtypeStruct((2, slots, head), jnp.bfloat16),
            jax.ShapeDtypeStruct((2, nx, ny, head), jnp.int32),
        ),
        in_specs=[whole(pltpu.SMEM)] * 2 + [whole()] * 4,
        out_specs=(whole(), whole()),
        compiler_params=params(16),
        name="make_keys",
    )(place, count, rows, mine, other, gain.reshape(1, head))


def queries_kernel(
    place_ref, rows_hbm, mine_hbm, other_hbm, gain_ref, out_ref, gate_ref, rows, weights, rows_here, weights_here
):
    parts, nx, _, deep, width = weights.shape
    slots, head = gate_ref.shape
    core = place_ref[0]
    rows_copies, weights_copies = [], []
    for part in range(parts):
        rows_copies.append(pltpu.make_async_copy(rows_hbm.at[part], rows.at[part], rows_here.at[part]))
        rows_copies[part].start()
    for part in range(parts):
        weights_copies.append(
            [
                pltpu.make_async_copy(source.at[:, part], weights.at[part, :, side], weights_here.at[which, part])
                for which, (source, side) in enumerate(((mine_hbm, core), (other_hbm, 1 - core)))
            ]
        )
        for copy in weights_copies[part]:
            copy.start()
    for copy in rows_copies:
        copy.wait()
    scale = norm_scale(rows, slots)
    routed = jnp.zeros((slots, rows.shape[2]), jnp.float32)
    total = jnp.zeros((slots, width), jnp.float32)
    for part in range(parts):
        block, router = normed_part(rows, part, slots, scale)
        routed += block.astype(jnp.float32) * router
        for copy in weights_copies[part]:
            copy.wait()
        total += dot(block, weights[part].reshape(nx * 2 * deep, width))
    gate = jax.nn.sigmoid(jnp.sum(routed, axis=-1, keepdims=True))
    gate_ref[...] = jnp.broadcast_to(gate, gate_ref.shape)
    for h in range(0, width, head):
        out_ref[:, h : h + head] = head_norm(total[:, h : h + head], gain_ref[...])


def make_queries(place, rows, mine, other, gain, slots):
    nx, parts, deep, width = mine.shape
    head = gain.shape[0]
    return pl.pallas_call(
        queries_kernel,
        out_shape=(
            jax.ShapeDtypeStruct((slots, width), jnp.bfloat16),
            jax.ShapeDtypeStruct((slots, head), jnp.float32),
        ),
        in_specs=[whole(pltpu.SMEM)] + [whole(pl.ANY)] * 3 + [whole()],
        out_specs=(whole(), whole()),
        scratch_shapes=[
            pltpu.VMEM(rows.shape, jnp.bfloat16),
            pltpu.VMEM((parts, nx, 2, deep, width), jnp.bfloat16),
            pltpu.SemaphoreType.DMA((parts,)),
            pltpu.SemaphoreType.DMA((2, parts)),
        ],
        compiler_params=params(),
        name="make_queries",
    )(place, rows, mine, other, gain.reshape(1, -1))


def pack_kernel(
    place_ref, counts_ref, count_ref, mine_hbm, other_hbm, _, keys_ref, flags, table_ref, mine_ref, other_ref, here
):
    nx, ny, slots, head = mine_ref.shape
    copies = [
        [
            pltpu.make_async_copy(source.at[x], target.at[x], here.at[which, x])
            for which, (source, target) in enumerate(((mine_hbm, mine_ref), (other_hbm, other_ref)))
        ]
        for x in range(nx)
    ]
    for pair in copies:
        for copy in pair:
            copy.start()
    core, shard = place_ref[0], place_ref[1]
    fill = lax.broadcasted_iota(jnp.int32, (slots, head), 0)

    end = jnp.int32(0)
    for x in range(nx):
        for copy in copies[x]:
            copy.wait()
        for y in range(ny):
            for which, ref in enumerate((mine_ref, other_ref)):
                side = jnp.where(core == 0, which, 1 - which)
                earlier = (y * nx + x) * 2 + side < shard
                length = jnp.where(earlier, counts_ref[which, x, y, 0], 0)
                table_ref[which, x * ny + y] = jnp.where(length > 0, end, -1)

                @pl.when(length > 0)
                def _():
                    where = pl.ds(pl.multiple_of(end, 16), slots)
                    keys_ref[where, :] = ref[x, y]
                    flags[where, :] = jnp.where(fill < length, 1.0, 0.0).astype(jnp.bfloat16)

                end = end + (length + 15) // 16 * 16
        table_ref[2, 3 + x] = end
    table_ref[2, 0] = end
    table_ref[2, 1] = core
    table_ref[2, 2] = count_ref[0]
    rest = pl.ds(pl.multiple_of(end, 16), TILE)
    keys_ref[rest, :] = jnp.zeros((TILE, head), jnp.bfloat16)
    flags[rest, :] = jnp.zeros((TILE, head), jnp.bfloat16)


def packed_rows(sources, block):
    return -(-(sources * block // 8 + 16 * sources) // TILE) * TILE


def pack_keys(place, counts, count, mine, other, after, block):
    nx, ny, _, head = mine.shape
    rows = packed_rows(2 * nx * ny, block)
    return pl.pallas_call(
        pack_kernel,
        out_shape=(
            jax.ShapeDtypeStruct((rows + TILE, head), jnp.bfloat16),
            jax.ShapeDtypeStruct((rows + TILE, head), jnp.bfloat16),
            jax.ShapeDtypeStruct((3, nx * ny), jnp.int32),
        ),
        in_specs=[whole(pltpu.SMEM)] * 3 + [whole(pl.ANY)] * 3,
        out_specs=(whole(), whole(), whole(pltpu.SMEM)),
        scratch_shapes=[
            pltpu.VMEM(mine.shape, jnp.bfloat16),
            pltpu.VMEM(other.shape, jnp.bfloat16),
            pltpu.SemaphoreType.DMA((2, nx)),
        ],
        compiler_params=params(),
        name="pack_keys",
    )(place, counts, count, mine, other, after)


def attend_kernel(
    table_ref, q_ref, own_ref, pos_row_ref, gate_ref, keys_hbm, flags_hbm, values_hbm,
    out_ref, keys_ref, values, packed, total, arrived, chunks,
):
    nx, _, ny, slots, head = values.shape
    group = q_ref.shape[1] // head
    end, core, count = table_ref[2, 0], table_ref[2, 1], table_ref[2, 2]
    factor = math.log2(math.e) / math.sqrt(head)
    copies = [pltpu.make_async_copy(values_hbm.at[x], values.at[x], arrived.at[x]) for x in range(nx)]
    pieces_used = (end + PIECE - 1) // PIECE
    full, tail = pieces_used // (TILE // PIECE), pieces_used % (TILE // PIECE)

    def chunk(at):
        rows = pl.ds(pl.multiple_of(at * TILE, TILE), TILE)
        return (
            pltpu.make_async_copy(keys_hbm.at[rows, :], keys_ref.at[rows, :], chunks.at[0, at]),
            pltpu.make_async_copy(flags_hbm.at[rows, :], packed.at[rows, head:], chunks.at[1, at]),
        )

    def begin(at, carry):
        for copy in chunk(at):
            copy.start()
        return carry

    copies[0].start()
    lax.fori_loop(0, (end + TILE - 1) // TILE, begin, 0)
    for copy in copies[1:]:
        copy.start()

    across = lax.broadcasted_iota(jnp.int32, (slots, slots), 1)
    along = lax.broadcasted_iota(jnp.int32, (slots, slots), 0)
    positions = jnp.broadcast_to(pos_row_ref[...].astype(jnp.float32), (slots, slots))
    mine = jnp.sum(jnp.where(across == along, positions, 0.0), axis=1, keepdims=True)
    allowed = (positions <= mine) & (across < count)
    summed = jnp.concatenate([own_ref[1], jnp.ones((slots, head), jnp.bfloat16)], axis=1)
    for h in range(group):
        query = q_ref[:, h * head : (h + 1) * head]
        weights = jnp.exp2(dot(query, own_ref[0], 1, 1) * factor)
        total[h] = dot(jnp.where(allowed, weights, 0.0).astype(jnp.bfloat16), summed)

    def weigh(start, size):
        rows = pl.ds(pl.multiple_of(start, size), size)
        keys, vals = keys_ref[rows, :], packed[rows, :]
        for h in range(group):
            query = q_ref[:, h * head : (h + 1) * head]
            weights = jnp.exp2(dot(query, keys, 1, 1) * factor).astype(jnp.bfloat16)
            total[h] += dot(weights, vals)

    def tile(at, carry):
        for copy in chunk(at):
            copy.wait()
        weigh(at * TILE, TILE)
        return carry

    done = jnp.int32(0)
    for x in range(nx):
        copies[x].wait()
        for y in range(ny):
            for which in range(2):
                offset = table_ref[which, x * ny + y]

                @pl.when(offset >= 0)
                def _():
                    side = jnp.where(core == 0, which, 1 - which)
                    packed[pl.ds(pl.multiple_of(offset, 16), slots), :head] = values[x, side, y]

        if x == nx - 1:
            packed[pl.ds(pl.multiple_of(end, 16), TILE), :head] = jnp.zeros((TILE, head), jnp.bfloat16)
        ready = full if x == nx - 1 else table_ref[2, 3 + x] // TILE
        lax.fori_loop(done, ready, tile, 0)
        done = ready

    @pl.when(tail > 0)
    def _():
        for copy in chunk(done):
            copy.wait()

    for size in (2 * PIECE, PIECE):

        @pl.when((tail * PIECE) & size > 0)
        def _():
            weigh(done * TILE + ((tail * PIECE) // (2 * size) * (2 * size)), size)

    block = out_ref.shape[0]
    live = lax.broadcasted_iota(jnp.int32, (slots, 1), 0) < count
    pieces = []
    for h in range(group):
        sums = total[h]
        scale = jnp.where(live, gate_ref[...] / jnp.where(live, sums[:, head:], 1.0), 0.0)
        pieces.append((sums[:, :head] * scale).astype(jnp.bfloat16))
    hit = (lax.broadcasted_iota(jnp.int32, (block, slots), 0) == pos_row_ref[...]) & (
        lax.broadcasted_iota(jnp.int32, (block, slots), 1) < count
    )
    one_hot = jnp.where(hit, 1.0, 0.0).astype(jnp.bfloat16)
    out_ref[...] = dot(one_hot, jnp.concatenate(pieces, axis=1)).astype(jnp.bfloat16)


def attend(table, queries, own, keys, flags, route_pos, gate, values, block):
    slots, width = queries.shape
    head = gate.shape[1]
    group = width // head
    return pl.pallas_call(
        attend_kernel,
        out_shape=jax.ShapeDtypeStruct((block, width), jnp.bfloat16),
        in_specs=[whole(pltpu.SMEM)] + [whole()] * 4 + [whole(pltpu.HBM)] * 3,
        out_specs=whole(),
        scratch_shapes=[
            pltpu.VMEM(keys.shape, jnp.bfloat16),
            pltpu.VMEM(values.shape, jnp.bfloat16),
            pltpu.VMEM((keys.shape[0], 2 * head), jnp.bfloat16),
            pltpu.VMEM((group, slots, 2 * head), jnp.float32),
            pltpu.SemaphoreType.DMA((values.shape[0],)),
            pltpu.SemaphoreType.DMA((2, keys.shape[0] // TILE)),
        ],
        compiler_params=params(),
        name="attend",
    )(table, queries, own, route_pos.reshape(1, slots), gate, keys, flags, values)


def to_all(block, axes, peers):
    return lax.all_to_all(
        jnp.broadcast_to(block[None], (peers,) + block.shape), axes, 0, 0, tiled=True
    )


def swap_cores(block):
    return lax.ppermute(block, "core", [(0, 1), (1, 0)])


def local(
    tokens, x_gain, w_router, w_query, key_weight, value_weight, q_gain, key_norm_gain, route_pos, route_count
):
    ny, nx = lax.axis_size("y"), lax.axis_size("x")
    block = tokens.shape[0]
    slots = route_pos.shape[0]
    place = jnp.stack([lax.axis_index("core"), lax.axis_index(SEQ)]).astype(jnp.int32)
    deep, width = w_query.shape
    head = q_gain.shape[0]

    picked, weights = stage(
        route_count, tokens, route_pos, x_gain, w_router, w_query, key_weight, value_weight
    )
    rows = lax.all_gather(picked, "z", axis=0, tiled=False)

    weights_y = lax.all_gather(weights, "y", axis=0, tiled=False)
    kv_mine = to_all(weights_y[:, :, width:], "x", nx)
    kv_other = swap_cores(kv_mine)
    wq_mine = lax.all_gather(weights_y[:, :deep, :width], "x", axis=0, tiled=False)
    wq_other = swap_cores(wq_mine)

    own, counts = make_keys(place, route_count, rows, kv_mine, kv_other, key_norm_gain, slots)

    own_y = lax.all_gather(own.reshape(2 * slots, head), "y", axis=0, tiled=False)
    own_y = own_y.reshape(ny, 2, slots, head)
    values = lax.all_gather(own_y[:, 1], ("x", "core"), axis=0, tiled=False).reshape(nx, 2, ny, slots, head)
    mine = to_all(own_y[:, 0], "x", nx)
    other = swap_cores(mine)

    queries, gate = make_queries(place, rows, wq_mine, wq_other, q_gain, slots)
    keys, flags, table = pack_keys(place, counts, route_count, mine, other, queries, block)
    return attend(table, queries, own, keys, flags, route_pos, gate, values, block)


def solution(mesh):
    grid = Mesh(mesh.devices.reshape(8, 4, 2, 8), SEQ + ("z",))
    return jax.shard_map(
        local,
        mesh=grid,
        in_specs=(
            P(SEQ, "z"), P("z"), P("z"), P(SEQ, "z"), P(SEQ, "z"), P(SEQ, "z"), P(), P(), P(SEQ), P(SEQ),
        ),
        out_specs=P(SEQ, "z"),
        check_vma=False,
    )
```

```python
import math

import jax
import jax.numpy as jnp
from jax import lax
from jax.experimental import pallas as pl
from jax.experimental.pallas import tpu as pltpu
from jax.sharding import Mesh
from jax.sharding import PartitionSpec as P

SEQ = ("y", "x", "core")
TILE = 1024
PIECE = 256


def whole(memory_space=pltpu.VMEM):
    return pl.BlockSpec(memory_space=memory_space)


def params(mebibytes=56):
    return pltpu.CompilerParams(vmem_limit_bytes=mebibytes * 1024 * 1024)


def dot(a, b, contract_a=1, contract_b=0):
    return lax.dot_general(
        a, b, (((contract_a,), (contract_b,)), ((), ())), preferred_element_type=jnp.float32
    )


def stage_kernel(
    count_ref, tokens_ref, pos_ref, gain_ref, router_ref, query_ref, key_ref, value_ref, rows_ref, weights_ref
):
    slots = pos_ref.shape[1]
    block, width = tokens_ref.shape
    hit = lax.broadcasted_iota(jnp.int32, (block, slots), 0) == pos_ref[...]
    one_hot = jnp.where(hit, 1.0, 0.0).astype(jnp.bfloat16)
    rows_ref[:slots, :] = dot(one_hot, tokens_ref[...], 0, 0).astype(jnp.bfloat16)
    at = lax.broadcasted_iota(jnp.int32, (rows_ref.shape[0] - slots, width), 0)
    extra = jnp.where(at == 0, gain_ref[...].astype(jnp.float32).reshape(1, width), 0.0)
    extra = jnp.where(at == 1, router_ref[...].astype(jnp.float32).reshape(1, width), extra)
    rows_ref[slots:, :] = extra.astype(jnp.bfloat16)
    deep, query = query_ref.shape
    key = key_ref.shape[1]
    weights_ref[:deep, :query] = query_ref[...]
    weights_ref[:deep, query : query + key] = key_ref[...]
    weights_ref[:deep, query + key :] = value_ref[...]
    count = jnp.full((weights_ref.shape[0] - deep, weights_ref.shape[1]), count_ref[0], jnp.int32)
    weights_ref[deep:, :] = count.astype(jnp.float32).astype(jnp.bfloat16)


def stage(count, tokens, route_pos, x_gain, w_router, w_query, key_weight, value_weight):
    slots = route_pos.shape[0]
    width = tokens.shape[1]
    deep = w_query.shape[0]
    across = w_query.shape[1] + key_weight.shape[1] + value_weight.shape[1]
    return pl.pallas_call(
        stage_kernel,
        out_shape=(
            jax.ShapeDtypeStruct((slots + 8, width), jnp.bfloat16),
            jax.ShapeDtypeStruct((deep + 8, across), jnp.bfloat16),
        ),
        in_specs=[whole(pltpu.SMEM)] + [whole()] * 7,
        out_specs=(whole(), whole()),
        compiler_params=params(),
        name="stage",
    )(count, tokens, route_pos.reshape(1, slots), x_gain, w_router, w_query, key_weight, value_weight)


def head_norm(projected, gain):
    mean_sq = jnp.mean(projected * projected, axis=-1, keepdims=True)
    return (projected * lax.rsqrt(mean_sq + 1e-06) * gain).astype(jnp.bfloat16)


def in_feature_order(core, mine, other):
    even = jnp.where(core == 0, mine, other)
    odd = jnp.where(core == 0, other, mine)
    return jnp.stack([even, odd], axis=1).reshape(-1, mine.shape[-1])


def norm_scale(rows_ref, slots):
    parts, _, width = rows_ref.shape
    square = jnp.zeros((slots, width), jnp.float32)
    for part in range(parts):
        wide = rows_ref[part, :slots, :].astype(jnp.float32)
        square += wide * wide
    mean_sq = jnp.sum(square, axis=-1, keepdims=True) / (parts * width)
    return lax.rsqrt(mean_sq + 1e-05)


def normed_part(rows_ref, part, slots, scale):
    extra = rows_ref[part, slots:, :].astype(jnp.float32)
    wide = rows_ref[part, :slots, :].astype(jnp.float32)
    return (wide * scale * extra[0:1]).astype(jnp.bfloat16), extra[1:2]


def keys_kernel(place_ref, count_ref, rows_ref, mine_ref, other_ref, gain_ref, kv_ref, counts_ref):
    slots, head = kv_ref.shape[1:]
    nx, parts, _, both = mine_ref.shape
    deep = rows_ref.shape[2] // (2 * nx)
    core, count = place_ref[0], count_ref[0]
    scale = norm_scale(rows_ref, slots)
    total = jnp.zeros((slots, both), jnp.float32)
    for part in range(parts):
        block, _ = normed_part(rows_ref, part, slots, scale)
        weights = in_feature_order(core, mine_ref[:, part, :deep], other_ref[:, part, :deep])
        total += dot(block, weights)
    kv_ref[0] = head_norm(total[:, :head], gain_ref[...])
    live = lax.broadcasted_iota(jnp.int32, (slots, head), 0) < count
    kv_ref[1] = jnp.where(live, total[:, head:], 0.0).astype(jnp.bfloat16)
    for which, ref in enumerate((mine_ref, other_ref)):
        for x in range(nx):
            counts = jnp.max(ref[x, :, deep:, :head].astype(jnp.float32), axis=1)
            counts_ref[which, x] = counts.astype(jnp.int32)


def make_keys(place, count, rows, mine, other, gain, slots):
    nx, ny = mine.shape[:2]
    head = gain.shape[0]
    return pl.pallas_call(
        keys_kernel,
        out_shape=(
            jax.ShapeDtypeStruct((2, slots, head), jnp.bfloat16),
            jax.ShapeDtypeStruct((2, nx, ny, head), jnp.int32),
        ),
        in_specs=[whole(pltpu.SMEM)] * 2 + [whole()] * 4,
        out_specs=(whole(), whole()),
        compiler_params=params(16),
        name="make_keys",
    )(place, count, rows, mine, other, gain.reshape(1, head))


def queries_kernel(
    place_ref, rows_hbm, mine_hbm, other_hbm, gain_ref, out_ref, gate_ref, rows, weights, rows_here, weights_here
):
    parts, nx, _, deep, width = weights.shape
    slots, head = gate_ref.shape
    core = place_ref[0]
    rows_copies, weights_copies = [], []
    for part in range(parts):
        rows_copies.append(pltpu.make_async_copy(rows_hbm.at[part], rows.at[part], rows_here.at[part]))
        rows_copies[part].start()
    for part in range(parts):
        weights_copies.append(
            [
                pltpu.make_async_copy(source.at[:, part], weights.at[part, :, side], weights_here.at[which, part])
                for which, (source, side) in enumerate(((mine_hbm, core), (other_hbm, 1 - core)))
            ]
        )
        for copy in weights_copies[part]:
            copy.start()
    for copy in rows_copies:
        copy.wait()
    scale = norm_scale(rows, slots)
    routed = jnp.zeros((slots, rows.shape[2]), jnp.float32)
    total = jnp.zeros((slots, width), jnp.float32)
    for part in range(parts):
        block, router = normed_part(rows, part, slots, scale)
        routed += block.astype(jnp.float32) * router
        for copy in weights_copies[part]:
            copy.wait()
        total += dot(block, weights[part].reshape(nx * 2 * deep, width))
    gate = jax.nn.sigmoid(jnp.sum(routed, axis=-1, keepdims=True))
    gate_ref[...] = jnp.broadcast_to(gate, gate_ref.shape)
    for h in range(0, width, head):
        out_ref[:, h : h + head] = head_norm(total[:, h : h + head], gain_ref[...])


def make_queries(place, rows, mine, other, gain, slots):
    nx, parts, deep, width = mine.shape
    head = gain.shape[0]
    return pl.pallas_call(
        queries_kernel,
        out_shape=(
            jax.ShapeDtypeStruct((slots, width), jnp.bfloat16),
            jax.ShapeDtypeStruct((slots, head), jnp.float32),
        ),
        in_specs=[whole(pltpu.SMEM)] + [whole(pl.ANY)] * 3 + [whole()],
        out_specs=(whole(), whole()),
        scratch_shapes=[
            pltpu.VMEM(rows.shape, jnp.bfloat16),
            pltpu.VMEM((parts, nx, 2, deep, width), jnp.bfloat16),
            pltpu.SemaphoreType.DMA((parts,)),
            pltpu.SemaphoreType.DMA((2, parts)),
        ],
        compiler_params=params(),
        name="make_queries",
    )(place, rows, mine, other, gain.reshape(1, -1))


def pack_kernel(
    place_ref, counts_ref, count_ref, mine_hbm, other_hbm, _, keys_ref, flags, table_ref, mine_ref, other_ref, here
):
    nx, ny, slots, head = mine_ref.shape
    copies = [
        [
            pltpu.make_async_copy(source.at[x], target.at[x], here.at[which, x])
            for which, (source, target) in enumerate(((mine_hbm, mine_ref), (other_hbm, other_ref)))
        ]
        for x in range(nx)
    ]
    for pair in copies:
        for copy in pair:
            copy.start()
    core, shard = place_ref[0], place_ref[1]
    fill = lax.broadcasted_iota(jnp.int32, (slots, head), 0)

    end = jnp.int32(0)
    for x in range(nx):
        for copy in copies[x]:
            copy.wait()
        for y in range(ny):
            for which, ref in enumerate((mine_ref, other_ref)):
                side = jnp.where(core == 0, which, 1 - which)
                earlier = (y * nx + x) * 2 + side < shard
                length = jnp.where(earlier, counts_ref[which, x, y, 0], 0)
                table_ref[which, x * ny + y] = jnp.where(length > 0, end, -1)

                @pl.when(length > 0)
                def _():
                    where = pl.ds(pl.multiple_of(end, 16), slots)
                    keys_ref[where, :] = ref[x, y]
                    flags[where, :] = jnp.where(fill < length, 1.0, 0.0).astype(jnp.bfloat16)

                end = end + (length + 15) // 16 * 16
        table_ref[2, 3 + x] = end
    table_ref[2, 0] = end
    table_ref[2, 1] = core
    table_ref[2, 2] = count_ref[0]
    rest = pl.ds(pl.multiple_of(end, 16), TILE)
    keys_ref[rest, :] = jnp.zeros((TILE, head), jnp.bfloat16)
    flags[rest, :] = jnp.zeros((TILE, head), jnp.bfloat16)


def packed_rows(sources, block):
    return -(-(sources * block // 8 + 16 * sources) // TILE) * TILE


def pack_keys(place, counts, count, mine, other, after, block):
    nx, ny, _, head = mine.shape
    rows = packed_rows(2 * nx * ny, block)
    return pl.pallas_call(
        pack_kernel,
        out_shape=(
            jax.ShapeDtypeStruct((rows + TILE, head), jnp.bfloat16),
            jax.ShapeDtypeStruct((rows + TILE, head), jnp.bfloat16),
            jax.ShapeDtypeStruct((3, nx * ny), jnp.int32),
        ),
        in_specs=[whole(pltpu.SMEM)] * 3 + [whole(pl.ANY)] * 3,
        out_specs=(whole(), whole(), whole(pltpu.SMEM)),
        scratch_shapes=[
            pltpu.VMEM(mine.shape, jnp.bfloat16),
            pltpu.VMEM(other.shape, jnp.bfloat16),
            pltpu.SemaphoreType.DMA((2, nx)),
        ],
        compiler_params=params(),
        name="pack_keys",
    )(place, counts, count, mine, other, after)


def attend_kernel(
    table_ref, q_ref, own_ref, pos_row_ref, gate_ref, keys_hbm, flags_hbm, values_hbm,
    out_ref, keys_ref, values, packed, total, arrived, chunks,
):
    nx, _, ny, slots, head = values.shape
    group = q_ref.shape[1] // head
    end, core, count = table_ref[2, 0], table_ref[2, 1], table_ref[2, 2]
    factor = math.log2(math.e) / math.sqrt(head)
    copies = [pltpu.make_async_copy(values_hbm.at[x], values.at[x], arrived.at[x]) for x in range(nx)]
    pieces_used = (end + PIECE - 1) // PIECE
    full, tail = pieces_used // (TILE // PIECE), pieces_used % (TILE // PIECE)

    def chunk(at):
        rows = pl.ds(pl.multiple_of(at * TILE, TILE), TILE)
        return (
            pltpu.make_async_copy(keys_hbm.at[rows, :], keys_ref.at[rows, :], chunks.at[0, at]),
            pltpu.make_async_copy(flags_hbm.at[rows, :], packed.at[rows, head:], chunks.at[1, at]),
        )

    def begin(at, carry):
        for copy in chunk(at):
            copy.start()
        return carry

    tiles = (end + TILE - 1) // TILE
    copies[0].start()
    lax.fori_loop(0, jnp.minimum(tiles, 1), begin, 0)
    copies[1].start()

    across = lax.broadcasted_iota(jnp.int32, (slots, slots), 1)
    along = lax.broadcasted_iota(jnp.int32, (slots, slots), 0)
    positions = jnp.broadcast_to(pos_row_ref[...].astype(jnp.float32), (slots, slots))
    mine = jnp.sum(jnp.where(across == along, positions, 0.0), axis=1, keepdims=True)
    allowed = (positions <= mine) & (across < count)
    summed = jnp.concatenate([own_ref[1], jnp.ones((slots, head), jnp.bfloat16)], axis=1)
    for h in range(group):
        query = q_ref[:, h * head : (h + 1) * head]
        weights = jnp.exp2(dot(query, own_ref[0], 1, 1) * factor)
        total[h] = dot(jnp.where(allowed, weights, 0.0).astype(jnp.bfloat16), summed)

    lax.fori_loop(1, tiles, begin, 0)
    for copy in copies[2:]:
        copy.start()

    def weigh(start, size):
        rows = pl.ds(pl.multiple_of(start, size), size)
        keys, vals = keys_ref[rows, :], packed[rows, :]
        for h in range(group):
            query = q_ref[:, h * head : (h + 1) * head]
            weights = jnp.exp2(dot(query, keys, 1, 1) * factor).astype(jnp.bfloat16)
            total[h] += dot(weights, vals)

    def tile(at, carry):
        for copy in chunk(at):
            copy.wait()
        weigh(at * TILE, TILE)
        return carry

    done = jnp.int32(0)
    for x in range(nx):
        copies[x].wait()
        for y in range(ny):
            for which in range(2):
                offset = table_ref[which, x * ny + y]

                @pl.when(offset >= 0)
                def _():
                    side = jnp.where(core == 0, which, 1 - which)
                    packed[pl.ds(pl.multiple_of(offset, 16), slots), :head] = values[x, side, y]

        if x == nx - 1:
            packed[pl.ds(pl.multiple_of(end, 16), TILE), :head] = jnp.zeros((TILE, head), jnp.bfloat16)
        ready = full if x == nx - 1 else table_ref[2, 3 + x] // TILE
        lax.fori_loop(done, ready, tile, 0)
        done = ready

    @pl.when(tail > 0)
    def _():
        for copy in chunk(done):
            copy.wait()

    for size in (2 * PIECE, PIECE):

        @pl.when((tail * PIECE) & size > 0)
        def _():
            weigh(done * TILE + ((tail * PIECE) // (2 * size) * (2 * size)), size)

    block = out_ref.shape[0]
    live = lax.broadcasted_iota(jnp.int32, (slots, 1), 0) < count
    pieces = []
    for h in range(group):
        sums = total[h]
        scale = jnp.where(live, gate_ref[...] / jnp.where(live, sums[:, head:], 1.0), 0.0)
        pieces.append((sums[:, :head] * scale).astype(jnp.bfloat16))
    hit = (lax.broadcasted_iota(jnp.int32, (block, slots), 0) == pos_row_ref[...]) & (
        lax.broadcasted_iota(jnp.int32, (block, slots), 1) < count
    )
    one_hot = jnp.where(hit, 1.0, 0.0).astype(jnp.bfloat16)
    out_ref[...] = dot(one_hot, jnp.concatenate(pieces, axis=1)).astype(jnp.bfloat16)


def attend(table, queries, own, keys, flags, route_pos, gate, values, block):
    slots, width = queries.shape
    head = gate.shape[1]
    group = width // head
    return pl.pallas_call(
        attend_kernel,
        out_shape=jax.ShapeDtypeStruct((block, width), jnp.bfloat16),
        in_specs=[whole(pltpu.SMEM)] + [whole()] * 4 + [whole(pltpu.HBM)] * 3,
        out_specs=whole(),
        scratch_shapes=[
            pltpu.VMEM(keys.shape, jnp.bfloat16),
            pltpu.VMEM(values.shape, jnp.bfloat16),
            pltpu.VMEM((keys.shape[0], 2 * head), jnp.bfloat16),
            pltpu.VMEM((group, slots, 2 * head), jnp.float32),
            pltpu.SemaphoreType.DMA((values.shape[0],)),
            pltpu.SemaphoreType.DMA((2, keys.shape[0] // TILE)),
        ],
        compiler_params=params(),
        name="attend",
    )(table, queries, own, route_pos.reshape(1, slots), gate, keys, flags, values)


def to_all(block, axes, peers):
    return lax.all_to_all(
        jnp.broadcast_to(block[None], (peers,) + block.shape), axes, 0, 0, tiled=True
    )


def swap_cores(block):
    return lax.ppermute(block, "core", [(0, 1), (1, 0)])


def local(
    tokens, x_gain, w_router, w_query, key_weight, value_weight, q_gain, key_norm_gain, route_pos, route_count
):
    ny, nx = lax.axis_size("y"), lax.axis_size("x")
    block = tokens.shape[0]
    slots = route_pos.shape[0]
    place = jnp.stack([lax.axis_index("core"), lax.axis_index(SEQ)]).astype(jnp.int32)
    deep, width = w_query.shape
    head = q_gain.shape[0]

    picked, weights = stage(
        route_count, tokens, route_pos, x_gain, w_router, w_query, key_weight, value_weight
    )
    rows = lax.all_gather(picked, "z", axis=0, tiled=False)

    weights_y = lax.all_gather(weights, "y", axis=0, tiled=False)
    kv_mine = to_all(weights_y[:, :, width:], "x", nx)
    kv_other = swap_cores(kv_mine)
    wq_mine = lax.all_gather(weights_y[:, :deep, :width], "x", axis=0, tiled=False)
    wq_other = swap_cores(wq_mine)

    own, counts = make_keys(place, route_count, rows, kv_mine, kv_other, key_norm_gain, slots)

    own_y = lax.all_gather(own.reshape(2 * slots, head), "y", axis=0, tiled=False)
    own_y = own_y.reshape(ny, 2, slots, head)
    values = lax.all_gather(own_y[:, 1], ("x", "core"), axis=0, tiled=False).reshape(nx, 2, ny, slots, head)
    mine = to_all(own_y[:, 0], "x", nx)
    other = swap_cores(mine)

    queries, gate = make_queries(place, rows, wq_mine, wq_other, q_gain, slots)
    keys, flags, table = pack_keys(place, counts, route_count, mine, other, queries, block)
    return attend(table, queries, own, keys, flags, route_pos, gate, values, block)


def solution(mesh):
    grid = Mesh(mesh.devices.reshape(8, 4, 2, 8), SEQ + ("z",))
    return jax.shard_map(
        local,
        mesh=grid,
        in_specs=(
            P(SEQ, "z"), P("z"), P("z"), P(SEQ, "z"), P(SEQ, "z"), P(SEQ, "z"), P(), P(), P(SEQ), P(SEQ),
        ),
        out_specs=P(SEQ, "z"),
        check_vma=False,
    )
```

```python
import math

import jax
import jax.numpy as jnp
from jax import lax
from jax.experimental import pallas as pl
from jax.experimental.pallas import tpu as pltpu
from jax.sharding import Mesh
from jax.sharding import PartitionSpec as P

SEQ = ("y", "x", "core")
TILE = 1024
PIECE = 256


def whole(memory_space=pltpu.VMEM):
    return pl.BlockSpec(memory_space=memory_space)


def params(mebibytes=56):
    return pltpu.CompilerParams(vmem_limit_bytes=mebibytes * 1024 * 1024)


def dot(a, b, contract_a=1, contract_b=0):
    return lax.dot_general(
        a, b, (((contract_a,), (contract_b,)), ((), ())), preferred_element_type=jnp.float32
    )


def stage_kernel(tokens_ref, pos_ref, gain_ref, router_ref, rows_ref):
    slots = pos_ref.shape[1]
    block, width = tokens_ref.shape
    hit = lax.broadcasted_iota(jnp.int32, (block, slots), 0) == pos_ref[...]
    one_hot = jnp.where(hit, 1.0, 0.0).astype(jnp.bfloat16)
    rows_ref[:slots, :] = dot(one_hot, tokens_ref[...], 0, 0).astype(jnp.bfloat16)
    at = lax.broadcasted_iota(jnp.int32, (rows_ref.shape[0] - slots, width), 0)
    extra = jnp.where(at == 0, gain_ref[...].astype(jnp.float32).reshape(1, width), 0.0)
    extra = jnp.where(at == 1, router_ref[...].astype(jnp.float32).reshape(1, width), extra)
    rows_ref[slots:, :] = extra.astype(jnp.bfloat16)


def stage(tokens, route_pos, x_gain, w_router):
    slots = route_pos.shape[0]
    width = tokens.shape[1]
    return pl.pallas_call(
        stage_kernel,
        out_shape=jax.ShapeDtypeStruct((slots + 8, width), jnp.bfloat16),
        in_specs=[whole()] * 4,
        out_specs=whole(),
        compiler_params=params(),
        name="stage",
    )(tokens, route_pos.reshape(1, slots), x_gain, w_router)


def head_norm(projected, gain):
    mean_sq = jnp.mean(projected * projected, axis=-1, keepdims=True)
    return (projected * lax.rsqrt(mean_sq + 1e-06) * gain).astype(jnp.bfloat16)


def in_feature_order(core, mine, other):
    even = jnp.where(core == 0, mine, other)
    odd = jnp.where(core == 0, other, mine)
    return jnp.stack([even, odd], axis=1).reshape(-1, mine.shape[-1])


def norm_scale(rows_ref, slots):
    parts, _, width = rows_ref.shape
    square = jnp.zeros((slots, width), jnp.float32)
    for part in range(parts):
        wide = rows_ref[part, :slots, :].astype(jnp.float32)
        square += wide * wide
    mean_sq = jnp.sum(square, axis=-1, keepdims=True) / (parts * width)
    return lax.rsqrt(mean_sq + 1e-05)


def normed_part(rows_ref, part, slots, scale):
    extra = rows_ref[part, slots:, :].astype(jnp.float32)
    wide = rows_ref[part, :slots, :].astype(jnp.float32)
    return (wide * scale * extra[0:1]).astype(jnp.bfloat16), extra[1:2]


def keys_kernel(place_ref, count_ref, rows_ref, mine_ref, other_ref, gain_ref, kv_ref, counts_ref):
    slots, head = kv_ref.shape[1:]
    nx, parts, _, both = mine_ref.shape
    deep = rows_ref.shape[2] // (2 * nx)
    core, count = place_ref[0], count_ref[0]
    scale = norm_scale(rows_ref, slots)
    total = jnp.zeros((slots, both), jnp.float32)
    for part in range(parts):
        block, _ = normed_part(rows_ref, part, slots, scale)
        weights = in_feature_order(core, mine_ref[:, part, :deep], other_ref[:, part, :deep])
        total += dot(block, weights)
    kv_ref[0] = head_norm(total[:, :head], gain_ref[...])
    live = lax.broadcasted_iota(jnp.int32, (slots, head), 0) < count
    kv_ref[1] = jnp.where(live, total[:, head:], 0.0).astype(jnp.bfloat16)
    for which, ref in enumerate((mine_ref, other_ref)):
        for x in range(nx):
            counts = jnp.max(ref[x, :, deep:, :head].astype(jnp.float32), axis=1)
            counts_ref[which, x] = counts.astype(jnp.int32)


def make_keys(place, count, rows, mine, other, gain, slots):
    nx, ny = mine.shape[:2]
    head = gain.shape[0]
    return pl.pallas_call(
        keys_kernel,
        out_shape=(
            jax.ShapeDtypeStruct((2, slots, head), jnp.bfloat16),
            jax.ShapeDtypeStruct((2, nx, ny, head), jnp.int32),
        ),
        in_specs=[whole(pltpu.SMEM)] * 2 + [whole()] * 4,
        out_specs=(whole(), whole()),
        compiler_params=params(16),
        name="make_keys",
    )(place, count, rows, mine, other, gain.reshape(1, head))


def queries_kernel(
    place_ref, rows_hbm, mine_hbm, other_hbm, gain_ref, out_ref, gate_ref, rows, weights, rows_here, weights_here
):
    parts, nx, _, deep, width = weights.shape
    slots, head = gate_ref.shape
    core = place_ref[0]
    rows_copies, weights_copies = [], []
    for part in range(parts):
        rows_copies.append(pltpu.make_async_copy(rows_hbm.at[part], rows.at[part], rows_here.at[part]))
        rows_copies[part].start()
    for part in range(parts):
        weights_copies.append(
            [
                pltpu.make_async_copy(source.at[:, part], weights.at[part, :, side], weights_here.at[which, part])
                for which, (source, side) in enumerate(((mine_hbm, core), (other_hbm, 1 - core)))
            ]
        )
        for copy in weights_copies[part]:
            copy.start()
    for copy in rows_copies:
        copy.wait()
    scale = norm_scale(rows, slots)
    routed = jnp.zeros((slots, rows.shape[2]), jnp.float32)
    total = jnp.zeros((slots, width), jnp.float32)
    for part in range(parts):
        block, router = normed_part(rows, part, slots, scale)
        routed += block.astype(jnp.float32) * router
        for copy in weights_copies[part]:
            copy.wait()
        total += dot(block, weights[part].reshape(nx * 2 * deep, width))
    gate = jax.nn.sigmoid(jnp.sum(routed, axis=-1, keepdims=True))
    gate_ref[...] = jnp.broadcast_to(gate, gate_ref.shape)
    for h in range(0, width, head):
        out_ref[:, h : h + head] = head_norm(total[:, h : h + head], gain_ref[...])


def make_queries(place, rows, mine, other, gain, slots):
    nx, parts, deep, width = mine.shape
    head = gain.shape[0]
    return pl.pallas_call(
        queries_kernel,
        out_shape=(
            jax.ShapeDtypeStruct((slots, width), jnp.bfloat16),
            jax.ShapeDtypeStruct((slots, head), jnp.float32),
        ),
        in_specs=[whole(pltpu.SMEM)] + [whole(pl.ANY)] * 3 + [whole()],
        out_specs=(whole(), whole()),
        scratch_shapes=[
            pltpu.VMEM(rows.shape, jnp.bfloat16),
            pltpu.VMEM((parts, nx, 2, deep, width), jnp.bfloat16),
            pltpu.SemaphoreType.DMA((parts,)),
            pltpu.SemaphoreType.DMA((2, parts)),
        ],
        compiler_params=params(),
        name="make_queries",
    )(place, rows, mine, other, gain.reshape(1, -1))


def pack_kernel(
    place_ref, counts_ref, count_ref, mine_hbm, other_hbm, _, keys_ref, flags, table_ref, mine_ref, other_ref, here
):
    nx, ny, slots, head = mine_ref.shape
    copies = [
        [
            pltpu.make_async_copy(source.at[x], target.at[x], here.at[which, x])
            for which, (source, target) in enumerate(((mine_hbm, mine_ref), (other_hbm, other_ref)))
        ]
        for x in range(nx)
    ]
    for pair in copies:
        for copy in pair:
            copy.start()
    core, shard = place_ref[0], place_ref[1]
    fill = lax.broadcasted_iota(jnp.int32, (slots, head), 0)

    end = jnp.int32(0)
    for x in range(nx):
        for copy in copies[x]:
            copy.wait()
        for y in range(ny):
            for which, ref in enumerate((mine_ref, other_ref)):
                side = jnp.where(core == 0, which, 1 - which)
                earlier = (y * nx + x) * 2 + side < shard
                length = jnp.where(earlier, counts_ref[which, x, y, 0], 0)
                table_ref[which, x * ny + y] = jnp.where(length > 0, end, -1)

                @pl.when(length > 0)
                def _():
                    where = pl.ds(pl.multiple_of(end, 16), slots)
                    keys_ref[where, :] = ref[x, y]
                    flags[where, :] = jnp.where(fill < length, 1.0, 0.0).astype(jnp.bfloat16)

                end = end + (length + 15) // 16 * 16
        table_ref[2, 3 + x] = end
    table_ref[2, 0] = end
    table_ref[2, 1] = core
    table_ref[2, 2] = count_ref[0]
    rest = pl.ds(pl.multiple_of(end, 16), TILE)
    keys_ref[rest, :] = jnp.zeros((TILE, head), jnp.bfloat16)
    flags[rest, :] = jnp.zeros((TILE, head), jnp.bfloat16)


def packed_rows(sources, block):
    return -(-(sources * block // 8 + 16 * sources) // TILE) * TILE


def pack_keys(place, counts, count, mine, other, after, block):
    nx, ny, _, head = mine.shape
    rows = packed_rows(2 * nx * ny, block)
    return pl.pallas_call(
        pack_kernel,
        out_shape=(
            jax.ShapeDtypeStruct((rows + TILE, head), jnp.bfloat16),
            jax.ShapeDtypeStruct((rows + TILE, head), jnp.bfloat16),
            jax.ShapeDtypeStruct((3, nx * ny), jnp.int32),
        ),
        in_specs=[whole(pltpu.SMEM)] * 3 + [whole(pl.ANY)] * 3,
        out_specs=(whole(), whole(), whole(pltpu.SMEM)),
        scratch_shapes=[
            pltpu.VMEM(mine.shape, jnp.bfloat16),
            pltpu.VMEM(other.shape, jnp.bfloat16),
            pltpu.SemaphoreType.DMA((2, nx)),
        ],
        compiler_params=params(),
        name="pack_keys",
    )(place, counts, count, mine, other, after)


def attend_kernel(
    table_ref, q_ref, own_ref, pos_row_ref, gate_ref, keys_hbm, flags_hbm, values_hbm,
    out_ref, keys_ref, values, packed, total, arrived, chunks,
):
    nx, _, ny, slots, head = values.shape
    group = q_ref.shape[1] // head
    end, core, count = table_ref[2, 0], table_ref[2, 1], table_ref[2, 2]
    factor = math.log2(math.e) / math.sqrt(head)
    copies = [pltpu.make_async_copy(values_hbm.at[x], values.at[x], arrived.at[x]) for x in range(nx)]
    pieces_used = (end + PIECE - 1) // PIECE
    full, tail = pieces_used // (TILE // PIECE), pieces_used % (TILE // PIECE)

    def chunk(at):
        rows = pl.ds(pl.multiple_of(at * TILE, TILE), TILE)
        return (
            pltpu.make_async_copy(keys_hbm.at[rows, :], keys_ref.at[rows, :], chunks.at[0, at]),
            pltpu.make_async_copy(flags_hbm.at[rows, :], packed.at[rows, head:], chunks.at[1, at]),
        )

    def begin(at, carry):
        for copy in chunk(at):
            copy.start()
        return carry

    tiles = (end + TILE - 1) // TILE
    copies[0].start()
    lax.fori_loop(0, jnp.minimum(tiles, 1), begin, 0)
    copies[1].start()

    across = lax.broadcasted_iota(jnp.int32, (slots, slots), 1)
    along = lax.broadcasted_iota(jnp.int32, (slots, slots), 0)
    positions = jnp.broadcast_to(pos_row_ref[...].astype(jnp.float32), (slots, slots))
    mine = jnp.sum(jnp.where(across == along, positions, 0.0), axis=1, keepdims=True)
    allowed = (positions <= mine) & (across < count)
    summed = jnp.concatenate([own_ref[1], jnp.ones((slots, head), jnp.bfloat16)], axis=1)
    for h in range(group):
        query = q_ref[:, h * head : (h + 1) * head]
        weights = jnp.exp2(dot(query, own_ref[0], 1, 1) * factor)
        total[h] = dot(jnp.where(allowed, weights, 0.0).astype(jnp.bfloat16), summed)

    lax.fori_loop(1, tiles, begin, 0)
    for copy in copies[2:]:
        copy.start()

    def weigh(start, size):
        rows = pl.ds(pl.multiple_of(start, size), size)
        keys, vals = keys_ref[rows, :], packed[rows, :]
        for h in range(group):
            query = q_ref[:, h * head : (h + 1) * head]
            weights = jnp.exp2(dot(query, keys, 1, 1) * factor).astype(jnp.bfloat16)
            total[h] += dot(weights, vals)

    def tile(at, carry):
        for copy in chunk(at):
            copy.wait()
        weigh(at * TILE, TILE)
        return carry

    done = jnp.int32(0)
    for x in range(nx):
        copies[x].wait()
        for y in range(ny):
            for which in range(2):
                offset = table_ref[which, x * ny + y]

                @pl.when(offset >= 0)
                def _():
                    side = jnp.where(core == 0, which, 1 - which)
                    packed[pl.ds(pl.multiple_of(offset, 16), slots), :head] = values[x, side, y]

        if x == nx - 1:
            packed[pl.ds(pl.multiple_of(end, 16), TILE), :head] = jnp.zeros((TILE, head), jnp.bfloat16)
        ready = full if x == nx - 1 else table_ref[2, 3 + x] // TILE
        lax.fori_loop(done, ready, tile, 0)
        done = ready

    @pl.when(tail > 0)
    def _():
        for copy in chunk(done):
            copy.wait()

    for size in (2 * PIECE, PIECE):

        @pl.when((tail * PIECE) & size > 0)
        def _():
            weigh(done * TILE + ((tail * PIECE) // (2 * size) * (2 * size)), size)

    block = out_ref.shape[0]
    live = lax.broadcasted_iota(jnp.int32, (slots, 1), 0) < count
    pieces = []
    for h in range(group):
        sums = total[h]
        scale = jnp.where(live, gate_ref[...] / jnp.where(live, sums[:, head:], 1.0), 0.0)
        pieces.append((sums[:, :head] * scale).astype(jnp.bfloat16))
    hit = (lax.broadcasted_iota(jnp.int32, (block, slots), 0) == pos_row_ref[...]) & (
        lax.broadcasted_iota(jnp.int32, (block, slots), 1) < count
    )
    one_hot = jnp.where(hit, 1.0, 0.0).astype(jnp.bfloat16)
    out_ref[...] = dot(one_hot, jnp.concatenate(pieces, axis=1)).astype(jnp.bfloat16)


def attend(table, queries, own, keys, flags, route_pos, gate, values, block):
    slots, width = queries.shape
    head = gate.shape[1]
    group = width // head
    return pl.pallas_call(
        attend_kernel,
        out_shape=jax.ShapeDtypeStruct((block, width), jnp.bfloat16),
        in_specs=[whole(pltpu.SMEM)] + [whole()] * 4 + [whole(pltpu.HBM)] * 3,
        out_specs=whole(),
        scratch_shapes=[
            pltpu.VMEM(keys.shape, jnp.bfloat16),
            pltpu.VMEM(values.shape, jnp.bfloat16),
            pltpu.VMEM((keys.shape[0], 2 * head), jnp.bfloat16),
            pltpu.VMEM((group, slots, 2 * head), jnp.float32),
            pltpu.SemaphoreType.DMA((values.shape[0],)),
            pltpu.SemaphoreType.DMA((2, keys.shape[0] // TILE)),
        ],
        compiler_params=params(),
        name="attend",
    )(table, queries, own, route_pos.reshape(1, slots), gate, keys, flags, values)


def to_all(block, axes, peers):
    return lax.all_to_all(
        jnp.broadcast_to(block[None], (peers,) + block.shape), axes, 0, 0, tiled=True
    )


def swap_cores(block):
    return lax.ppermute(block, "core", [(0, 1), (1, 0)])


def local(
    tokens, x_gain, w_router, w_query, key_weight, value_weight, q_gain, key_norm_gain, route_pos, route_count
):
    ny, nx = lax.axis_size("y"), lax.axis_size("x")
    block = tokens.shape[0]
    slots = route_pos.shape[0]
    place = jnp.stack([lax.axis_index("core"), lax.axis_index(SEQ)]).astype(jnp.int32)
    deep, width = w_query.shape
    head = q_gain.shape[0]

    picked = stage(tokens, route_pos, x_gain, w_router)
    weights = jnp.concatenate([w_query, key_weight, value_weight], axis=1)
    counted = jnp.full((8, weights.shape[1]), route_count[0].astype(jnp.bfloat16))
    weights = jnp.concatenate([weights, counted], axis=0)
    rows = lax.all_gather(picked, "z", axis=0, tiled=False)

    weights_y = lax.all_gather(weights, "y", axis=0, tiled=False)
    kv_mine = to_all(weights_y[:, :, width:], "x", nx)
    kv_other = swap_cores(kv_mine)
    wq_mine = lax.all_gather(weights_y[:, :deep, :width], "x", axis=0, tiled=False)
    wq_other = swap_cores(wq_mine)

    own, counts = make_keys(place, route_count, rows, kv_mine, kv_other, key_norm_gain, slots)

    own_y = lax.all_gather(own.reshape(2 * slots, head), "y", axis=0, tiled=False)
    own_y = own_y.reshape(ny, 2, slots, head)
    values = lax.all_gather(own_y[:, 1], ("x", "core"), axis=0, tiled=False).reshape(nx, 2, ny, slots, head)
    mine = to_all(own_y[:, 0], "x", nx)
    other = swap_cores(mine)

    queries, gate = make_queries(place, rows, wq_mine, wq_other, q_gain, slots)
    keys, flags, table = pack_keys(place, counts, route_count, mine, other, queries, block)
    return attend(table, queries, own, keys, flags, route_pos, gate, values, block)


def solution(mesh):
    grid = Mesh(mesh.devices.reshape(8, 4, 2, 8), SEQ + ("z",))
    return jax.shard_map(
        local,
        mesh=grid,
        in_specs=(
            P(SEQ, "z"), P("z"), P("z"), P(SEQ, "z"), P(SEQ, "z"), P(SEQ, "z"), P(), P(), P(SEQ), P(SEQ),
        ),
        out_specs=P(SEQ, "z"),
        check_vma=False,
    )
```
